512 devices in a mesh: dp: 32 (over y, x), mp: 16 (over z, core).
Axes of the slice: x: 4, y: 8, z: 8, core: 2. Of those that a mesh axis runs over, the one named last changes fastest.
Arguments:
- grads: bfloat16 [32, 448, 17920], P('dp', None, 'mp'), may hold values from -6 to 6
- errors: bfloat16 [32, 448, 17920], P('dp', None, 'mp'), may hold values from -3 to 3
- q_start: float32 [17920, 128], P('mp'), may hold values from -0.046875 to 0.046875
Outputs:
- approx: bfloat16 [448, 17920], P(None, 'mp')
- q_next: float32 [17920, 128], P('mp')
- error_next: bfloat16 [32, 448, 17920], P('dp', None, 'mp')
The draws below stay inside these ranges and needn't reach their ends.
All inputs are finite; a program needn't handle non-finite values.
Results may differ from the reference program's by a relative error of at most 0.0012.
Values sent between devices are 32-bit elements; how exact they have to be, the bound alone decides.
A program may use at most 64 MiB of HBM per device.

```python
import jax
import jax.numpy as jnp
from jax import lax

FF = 17920
RANK = 128
ROWS = 448
REPLICAS = 32


def steps_of(stream_key, extent, shards, low, largest):
    def one(dim, parts):
        heights = jax.random.uniform(jax.random.fold_in(jax.random.fold_in(stream_key, 6), dim), (parts,), jnp.float32, low / len(shards), largest / len(shards))
        return jnp.repeat(jnp.exp(heights), extent[dim] // parts).reshape((-1,) + (1,) * (len(extent) - dim - 1))

    gain = one(*shards[0])
    for cut in shards[1:]:
        gain = gain * one(*cut)
    return gain


def bell_draw(key, shape, width, bound, shards=(), held_as=jnp.bfloat16):
    entries = jax.random.normal(key, shape, jnp.float32) * width
    if len(shards) > 0:
        entries = steps_of(key, shape, shards, -0.22, 0.18) * entries
    return jnp.clip(entries, min=-bound, max=bound).astype(held_as)


def setup_inputs(seed: int = 0) -> dict:
    arg_keys = jax.random.split(jax.random.key(seed), 4)
    return {
        "grads": bell_draw(arg_keys[0], (REPLICAS, ROWS, FF), 1.0, 6.0, ((0, 32), (2, 16))),
        "errors": bell_draw(arg_keys[1], (REPLICAS, ROWS, FF), 0.5, 3.0, ((0, 32), (2, 16))),
        "q_start": bell_draw(arg_keys[2], (FF, RANK), FF ** -0.5, 0.046875, ((0, 16),), jnp.float32),
    }


def reference(grads, errors, q_start):
    highest = lax.Precision.HIGHEST

    def merged_of(index):
        return grads[index].astype(jnp.float32) + errors[index].astype(jnp.float32)

    def add_left(index, running):
        return running + jnp.dot(merged_of(index).astype(jnp.float32), q_start.astype(jnp.float32), precision=highest, preferred_element_type=jnp.float32)
    p_mean = lax.fori_loop(0, REPLICAS, add_left, jnp.zeros((ROWS, RANK), jnp.float32)) / REPLICAS
    gram_matrix = jnp.dot(p_mean.T.astype(jnp.float32), p_mean.astype(jnp.float32), precision=highest, preferred_element_type=jnp.float32)
    factor_low = jnp.linalg.cholesky(gram_matrix)
    p_hat = lax.linalg.triangular_solve(factor_low, p_mean, left_side=False, lower=True, transpose_a=True)

    def add_right(index, running):
        return running + jnp.dot(merged_of(index).T.astype(jnp.float32), p_hat.astype(jnp.float32), precision=highest, preferred_element_type=jnp.float32)
    q_next = lax.fori_loop(0, REPLICAS, add_right, jnp.zeros((FF, RANK), jnp.float32)) / REPLICAS
    full_approx = jnp.dot(p_hat.astype(jnp.float32), q_next.T.astype(jnp.float32), precision=highest, preferred_element_type=jnp.float32)

    def new_error(operands):
        return (operands[0].astype(jnp.float32) + operands[1].astype(jnp.float32) - full_approx).astype(jnp.bfloat16)
    error_next = lax.map(new_error, (grads, errors))
    return (full_approx.astype(jnp.bfloat16), q_next, error_next)
```

```python
import functools

import jax
import jax.numpy as jnp
from jax import lax
from jax.experimental import pallas as pl
from jax.experimental.pallas import tpu as pltpu
from jax.sharding import PartitionSpec as P

MESH = pl.DeviceIdType.MESH
F32 = jnp.float32
BF16 = jnp.bfloat16

NX, NY, NZ, NC = 4, 8, 8, 2
OWNERS = 7
PIECE = 40
SPLIT = 32


def far_first(n):
    return sorted(range(1, n), key=lambda k: -min(k, n - k))


def near_first(n):
    return sorted(range(1, n), key=lambda k: min(k, n - k))


def dot(a, b, dims=((1,), (0,)), precision=None):
    return lax.dot_general(a, b, (dims, ((), ())), precision=precision, preferred_element_type=F32)


def halves(a):
    high = a.astype(BF16)
    return high, (a - high.astype(F32)).astype(BF16)


def panels(c, first, last):
    n = c.shape[0]

    def panel(index, c):
        rows = lax.broadcasted_iota(jnp.int32, (n, 1), 0)
        lanes = lax.broadcasted_iota(jnp.int32, (1, n), 1)
        inside = rows < n - 8 * index
        for j in range(8):
            inverse = 1.0 / c[j : j + 1, j : j + 1]
            row = c[j : j + 1, :] * inverse
            row = jnp.where(lanes == j, inverse, row)
            column = jnp.where((rows > j) & inside, c[:, j : j + 1], 0.0)
            below = (rows > j) & inside & (lanes == j)
            c = jnp.where(below, 0.0, c) - column * row
        c = pltpu.roll(c, n - 8, 1)
        return jnp.concatenate([c[8:], c[:8]], axis=0)

    return lax.fori_loop(first, last, panel, c)


def inverse_factor(c):
    n = c.shape[0]
    rows = lax.broadcasted_iota(jnp.int32, (n, n), 0)
    lanes = lax.broadcasted_iota(jnp.int32, (n, n), 1)
    pivots = jnp.sum(jnp.where(rows == lanes, c, 0.0), axis=1, keepdims=True)
    return jnp.where(lanes < rows, c, jnp.where(rows == lanes, 1.0, 0.0)) * lax.rsqrt(pivots)


def exchange(
    g_hbm, e_hbm, q_hbm, right_out, p_hat_out, inverse_out,
    g_v, e_v, q_v, gt_v, et_v, part_v, a_rx, by_rx, bz_rx, dz_rx, dy_rx, mean_v,
    qp_v, rx_rx, ry_v, ry_rx, right_v, c_v,
    load_sem, a_s, a_r, by_s, by_r, bz_s, bz_r, dz_s, dz_r, dy_s, dy_r, c_s, c_r,
    rx_s, rx_r, ry_s, ry_r, gy_s, gy_r, gx_s, gx_r,
):
    rows, width = g_v.shape
    chunk = rows // (NX * NC)
    cols = width // NX
    dp = lax.axis_index("dp")
    mp = lax.axis_index("mp")
    y, x, z, core = dp // NX, dp % NX, mp // NC, mp % NC

    def device(y, x, z, core):
        return (y * NX + x, z * NC + core)

    pending = []

    def send(src, dst, s, r, to):
        copy = pltpu.make_async_remote_copy(
            src_ref=src, dst_ref=dst, send_sem=s, recv_sem=r, device_id=to, device_id_type=MESH
        )
        copy.start()
        return copy

    loads = [
        pltpu.make_async_copy(src, dst, load_sem.at[i])
        for i, (src, dst) in enumerate(((q_hbm, q_v), (g_hbm, g_v), (e_hbm, e_v)))
    ]
    for load in loads:
        load.start()

    xc_offsets = [(dx, dc) for dx in far_first(NX) + [0] for dc in reversed(range(NC)) if (dx, dc) != (0, 0)]
    barrier = pltpu.get_barrier_semaphore()
    others = (
        [device((y + k) % NY, x, z, core) for k in far_first(NY)]
        + [device(y, x, (z + k) % NZ, core) for k in far_first(NZ)]
        + [device(y, (x + dx) % NX, z, (core + dc) % NC) for dx, dc in xc_offsets]
    )
    for other in others:
        pl.semaphore_signal(barrier, inc=1, device_id=other, device_id_type=MESH)

    loads[0].wait()
    q2 = jnp.concatenate(halves(q_v[...]), axis=1)
    loads[1].wait()
    loads[2].wait()
    both = dot(g_v[...], q2) + dot(e_v[...], q2)
    rank = q_v.shape[1]
    part_v[...] = both[:, :rank] + both[:, rank:]
    pl.semaphore_wait(barrier, len(others))

    mine = x * NC + core
    for k, (dx, dc) in enumerate(xc_offsets):
        x2, c2 = (x + dx) % NX, (core + dc) % NC
        src = part_v.at[pl.ds(pl.multiple_of((x2 * NC + c2) * chunk, 8), chunk)]
        pending.append(send(src, a_rx.at[k], a_s.at[k], a_r.at[k], device(y, x2, z, c2)))

    for start in range(0, width, 128):
        stop = min(start + 128, width)
        gt_v[start:stop, :] = g_v[:, start:stop].T
        et_v[start:stop, :] = e_v[:, start:stop].T

    total = part_v[pl.ds(pl.multiple_of(mine * chunk, 8), chunk), :]
    for k in range(len(xc_offsets)):
        pltpu.make_async_copy(a_rx.at[k], a_rx.at[k], a_r.at[k]).wait()
        total = total + a_rx[k]

    def spread_y(ref, s, r, k):
        y2 = (y + k) % NY
        return send(ref.at[y], ref.at[y], s.at[k - 1], r.at[k - 1], device(y2, x, z, core))

    def spread_z(ref, s, r, k):
        z2 = (z + k) % NZ
        return send(ref.at[z], ref.at[z], s.at[k - 1], r.at[k - 1], device(y, x, z2, core))

    def collect(ref, r, n):
        for k in range(1, n):
            pltpu.make_async_copy(ref.at[0], ref.at[0], r.at[k - 1]).wait()
        value = ref[0]
        for k in range(1, n):
            value = value + ref[k]
        return value

    by_rx[y] = total[:SPLIT]
    bz_rx[z] = total[SPLIT:]
    for ky, kz in zip(far_first(NY), far_first(NZ)):
        pending.append(spread_y(by_rx, by_s, by_r, ky))
        pending.append(spread_z(bz_rx, bz_s, bz_r, kz))
    dz_rx[z] = collect(by_rx, by_r, NY)
    for kz in far_first(NZ):
        pending.append(spread_z(dz_rx, dz_s, dz_r, kz))
    dy_rx[y] = collect(bz_rx, bz_r, NZ)
    for ky in far_first(NY):
        pending.append(spread_y(dy_rx, dy_s, dy_r, ky))
    first = collect(dz_rx, dz_r, NZ)
    second = collect(dy_rx, dy_r, NY)

    replicas = NX * NY
    mean_v[pl.ds(pl.multiple_of(mine * chunk, 8), SPLIT), :] = first / replicas
    mean_v[pl.ds(pl.multiple_of(mine * chunk + SPLIT, 8), chunk - SPLIT), :] = second / replicas
    own = mean_v.at[pl.ds(pl.multiple_of(mine * chunk, 8), chunk)]
    for k, (dx, dc) in enumerate(xc_offsets):
        x2, c2 = (x + dx) % NX, (core + dc) % NC
        pending.append(send(own, own, c_s.at[k], c_r.at[k], device(y, x2, z, c2)))
    for k in range(len(xc_offsets)):
        pltpu.make_async_copy(own, own, c_r.at[k]).wait()

    mean = mean_v[...]
    p2 = jnp.concatenate(halves(mean), axis=1)
    both = dot(gt_v[...], p2) + dot(et_v[...], p2)
    qp_v[...] = both[:, :rank] + both[:, rank:]

    def piece(x, y):
        return pl.ds(pl.multiple_of(x * cols + y * PIECE, 8), PIECE)

    def local_piece(y):
        return pl.ds(pl.multiple_of(y * PIECE, 8), PIECE)

    x_offsets = far_first(NX)
    for ky in far_first(NY) + [0]:
        y2 = (y + ky) % NY

        @pl.when(y2 < OWNERS)
        def _():
            for kx in x_offsets:
                x2 = (x + kx) % NX
                send(
                    qp_v.at[piece(x2, y2)], rx_rx.at[kx - 1, local_piece(y2)],
                    rx_s.at[kx - 1, ky], rx_r.at[kx - 1, ky], device(y, x2, z, core),
                )

    gram = dot(mean, mean, ((0,), (0,)), lax.Precision.HIGHEST)
    steps = gram.shape[0] // 8
    cut1, cut2 = steps // 4, steps * 5 // 8
    c_v[...] = panels(gram, 0, cut1)

    for ky in far_first(NY) + [0]:
        y2 = (y + ky) % NY

        @pl.when(y2 < OWNERS)
        def _():
            value = qp_v[piece(x, y2), :]
            for kx in x_offsets:
                got = rx_rx.at[kx - 1, local_piece(y2)]
                pltpu.make_async_copy(got, got, rx_r.at[kx - 1, ky]).wait()
                value = value + got[...]
            ry_v[local_piece(y2), :] = value
            if ky:
                send(ry_v.at[local_piece(y2)], ry_rx.at[ky - 1], ry_s.at[ky - 1], ry_r.at[ky - 1], device(y2, x, z, core))

    c_v[...] = panels(c_v[...], cut1, cut2)

    @pl.when(y < OWNERS)
    def _():
        value = ry_v[local_piece(y), :]
        for ky in near_first(NY):
            pltpu.make_async_copy(ry_rx.at[ky - 1], ry_rx.at[ky - 1], ry_r.at[ky - 1]).wait()
            value = value + ry_rx[ky - 1]
        right_v[piece(x, y), :] = value / replicas
        own = right_v.at[piece(x, y)]
        for ky in far_first(NY):
            send(own, own, gy_s.at[ky - 1], gy_r.at[ky - 1], device((y + ky) % NY, x, z, core))
        for kx in x_offsets:
            send(own, own, gx_s.at[kx - 1, 0], gx_r.at[kx - 1, 0], device(y, (x + kx) % NX, z, core))

    c_v[...] = panels(c_v[...], cut2, steps)

    for ky in near_first(NY):
        y2 = (y + NY - ky) % NY

        @pl.when(y2 < OWNERS)
        def _():
            got = right_v.at[piece(x, y2)]
            pltpu.make_async_copy(got, got, gy_r.at[ky - 1]).wait()
            for kx in x_offsets:
                send(got, got, gx_s.at[kx - 1, ky], gx_r.at[kx - 1, ky], device(y, (x + kx) % NX, z, core))

    inverse = inverse_factor(c_v[...])
    inverse_out[...] = inverse
    p_hat_out[...] = dot(mean, inverse, ((1,), (1,)), lax.Precision.HIGHEST)

    for copy in pending:
        copy.wait_send()
    for ky in range(NY):
        here = (y + ky) % NY
        there = (y + NY - ky) % NY

        @pl.when(here < OWNERS)
        def _():
            out = qp_v.at[piece(x, here)]
            for kx in x_offsets:
                pltpu.make_async_copy(out, out, rx_s.at[kx - 1, ky]).wait()
            if ky:
                pltpu.make_async_copy(out, out, ry_s.at[ky - 1]).wait()

        @pl.when(there < OWNERS)
        def _():
            out = right_v.at[piece(x, there)]
            for kx in x_offsets:
                pltpu.make_async_copy(out, out, gx_r.at[kx - 1, ky]).wait()
                pltpu.make_async_copy(out, out, gx_s.at[kx - 1, ky]).wait()

    @pl.when(y < OWNERS)
    def _():
        out = right_v.at[piece(x, y)]
        for ky in range(1, NY):
            pltpu.make_async_copy(out, out, gy_s.at[ky - 1]).wait()

    right_out[...] = right_v[...]


def finish(
    g_v, e_v, right_v, p_hat_v, inverse_v, approx_hbm, q_hbm, error_hbm,
    q_v, approx_v, error_v, q_sem, sems,
):
    rows = g_v.shape[0]
    block = 112 if rows % 112 == 0 else rows
    inverse_high, inverse_low = halves(inverse_v[...])
    high, low = halves(right_v[...])
    q_next = dot(
        jnp.concatenate([high, low, high], axis=1),
        jnp.concatenate([inverse_high, inverse_high, inverse_low], axis=1),
        ((1,), (1,)),
    )
    q_v[...] = q_next
    q_copy = pltpu.make_async_copy(q_v, q_hbm, q_sem)
    q_copy.start()
    q_high, q_low = halves(q_next)
    q3 = jnp.concatenate([q_high, q_high, q_low], axis=1)
    copies = [q_copy]
    for i in range(rows // block):
        part = pl.ds(i * block, block)
        p_high, p_low = halves(p_hat_v[part, :])
        full = dot(jnp.concatenate([p_high, p_low, p_high], axis=1), q3, ((1,), (1,)))
        approx_v[part, :] = full.astype(BF16)
        error_v[part, :] = (g_v[part, :].astype(F32) + e_v[part, :].astype(F32) - full).astype(BF16)
        for k, (src, dst) in enumerate(((approx_v, approx_hbm), (error_v, error_hbm))):
            copy = pltpu.make_async_copy(src.at[part], dst.at[part], sems.at[k, i])
            copy.start()
            copies.append(copy)
    for copy in copies:
        copy.wait()


def local(grads, errors, q_start):
    grads, errors = grads[0], errors[0]
    rows, width = grads.shape
    rank = q_start.shape[1]
    chunk = rows // (NX * NC)
    cols = width // NX
    nxc = NX * NC - 1
    anywhere = pl.BlockSpec(memory_space=pl.ANY)
    vmem = pl.BlockSpec(memory_space=pltpu.VMEM)
    dma = pltpu.SemaphoreType.DMA
    right, p_hat, inverse = pl.pallas_call(
        exchange,
        out_shape=(
            jax.ShapeDtypeStruct((width, rank), F32),
            jax.ShapeDtypeStruct((rows, rank), F32),
            jax.ShapeDtypeStruct((rank, rank), F32),
        ),
        in_specs=[anywhere] * 3,
        out_specs=(vmem,) * 3,
        scratch_shapes=[
            pltpu.VMEM((rows, width), BF16),
            pltpu.VMEM((rows, width), BF16),
            pltpu.VMEM((width, rank), F32),
            pltpu.VMEM((width, rows), BF16),
            pltpu.VMEM((width, rows), BF16),
            pltpu.VMEM((rows, rank), F32),
            pltpu.VMEM((nxc, chunk, rank), F32),
            pltpu.VMEM((NY, SPLIT, rank), F32),
            pltpu.VMEM((NZ, chunk - SPLIT, rank), F32),
            pltpu.VMEM((NZ, SPLIT, rank), F32),
            pltpu.VMEM((NY, chunk - SPLIT, rank), F32),
            pltpu.VMEM((rows, rank), F32),
            pltpu.VMEM((width, rank), F32),
            pltpu.VMEM((NX - 1, cols, rank), F32),
            pltpu.VMEM((cols, rank), F32),
            pltpu.VMEM((NY - 1, PIECE, rank), F32),
            pltpu.VMEM((width, rank), F32),
            pltpu.VMEM((rank, rank), F32),
            dma((3,)),
            dma((nxc,)), dma((nxc,)),
            dma((NY - 1,)), dma((NY - 1,)),
            dma((NZ - 1,)), dma((NZ - 1,)),
            dma((NZ - 1,)), dma((NZ - 1,)),
            dma((NY - 1,)), dma((NY - 1,)),
            dma((nxc,)), dma((nxc,)),
            dma((NX - 1, NY)), dma((NX - 1, NY)),
            dma((NY - 1,)), dma((NY - 1,)),
            dma((NY - 1,)), dma((NY - 1,)),
            dma((NX - 1, NY)), dma((NX - 1, NY)),
        ],
        compiler_params=pltpu.CompilerParams(
            collective_id=0, has_side_effects=True, vmem_limit_bytes=24 * 2**20
        ),
        name="exchange",
    )(grads, errors, q_start)

    block = 112 if rows % 112 == 0 else rows
    approx, q_next, error_next = pl.pallas_call(
        finish,
        out_shape=(
            jax.ShapeDtypeStruct((rows, width), BF16),
            jax.ShapeDtypeStruct((width, rank), F32),
            jax.ShapeDtypeStruct((rows, width), BF16),
        ),
        in_specs=[vmem] * 5,
        out_specs=(anywhere,) * 3,
        scratch_shapes=[
            pltpu.VMEM((width, rank), F32),
            pltpu.VMEM((rows, width), BF16),
            pltpu.VMEM((rows, width), BF16),
            dma,
            dma((2, rows // block)),
        ],
        compiler_params=pltpu.CompilerParams(vmem_limit_bytes=24 * 2**20),
        name="finish",
    )(grads, errors, right, p_hat, inverse)
    return approx, q_next, error_next[None]


def solution(mesh):
    return jax.shard_map(
        local,
        mesh=mesh,
        in_specs=(P("dp", None, "mp"), P("dp", None, "mp"), P("mp", None)),
        out_specs=(P(None, "mp"), P("mp", None), P("dp", None, "mp")),
        check_vma=False,
    )
```

```python
import functools

import jax
import jax.numpy as jnp
from jax import lax
from jax.experimental import pallas as pl
from jax.experimental.pallas import tpu as pltpu
from jax.sharding import PartitionSpec as P

MESH = pl.DeviceIdType.MESH
F32 = jnp.float32
BF16 = jnp.bfloat16

NX, NY, NZ, NC = 4, 8, 8, 2
OWNERS = 7
PIECE = 40
SPLIT = 32
BLOCK = 112
TALL = 224
LIMIT = 53 * 2**20


def loop(n, body):
    def step(i, carry):
        body(i)
        return carry

    lax.fori_loop(0, n, step, 0)


def far_first(i, n):
    return n // 2 + (i + 1) // 2 * (1 - 2 * (i % 2))


def dot(a, b, dims=((1,), (0,)), precision=None):
    return lax.dot_general(a, b, (dims, ((), ())), precision=precision, preferred_element_type=F32)


def halves(a):
    high = a.astype(BF16)
    return high, (a - high.astype(F32)).astype(BF16)


def span(start, size, unit=8):
    return pl.ds(pl.multiple_of(start, unit), size)


def panel(index, c):
    n = c.shape[0]
    rows = lax.broadcasted_iota(jnp.int32, (n, 1), 0)
    lanes = lax.broadcasted_iota(jnp.int32, (1, n), 1)
    inside = rows < n - 8 * index
    for j in range(8):
        inverse = 1.0 / c[j : j + 1, j : j + 1]
        row = c[j : j + 1, :] * inverse
        row = jnp.where(lanes == j, inverse, row)
        below = (rows > j) & inside
        column = jnp.where(below, c[:, j : j + 1], 0.0)
        c = jnp.where(below & (lanes == j), 0.0, c) - column * row
    c = pltpu.roll(c, n - 8, 1)
    return jnp.concatenate([c[8:], c[:8]], axis=0)


def inverse_factor(c):
    n = c.shape[0]
    rows = lax.broadcasted_iota(jnp.int32, (n, n), 0)
    lanes = lax.broadcasted_iota(jnp.int32, (n, n), 1)
    pivots = jnp.sum(jnp.where(rows == lanes, c, 0.0), axis=1, keepdims=True)
    return jnp.where(lanes < rows, c, jnp.where(rows == lanes, 1.0, 0.0)) * lax.rsqrt(pivots)


def exchange(
    g_hbm, e_hbm, q_hbm, right_out, p_hat_out, inverse_out,
    m_v, q_v, t_v, part_v, a_rx, by_rx, bz_rx, dz_rx, dy_rx, mean_v, p2_v,
    qp_v, rx_rx, ry_v, ry_rx, right_v, c_v,
    load_sem, a_s, a_r, by_s, by_r, bz_s, bz_r, dz_s, dz_r, dy_s, dy_r, c_s, c_r,
    rx_s, rx_r, ry_s, ry_r, gy_s, gy_r, gx_s, gx_r,
):
    _, rows, width = m_v.shape
    rank = q_v.shape[1]
    chunk = rows // (NX * NC)
    cols = width // NX
    replicas = NX * NY
    dp = lax.axis_index("dp")
    mp = lax.axis_index("mp")
    y, x, z, core = dp // NX, dp % NX, mp // NC, mp % NC

    def device(y, x, z, core):
        return (y * NX + x, z * NC + core)

    def send(src, dst, s, r, to):
        pltpu.make_async_remote_copy(
            src_ref=src, dst_ref=dst, send_sem=s, recv_sem=r, device_id=to, device_id_type=MESH
        ).start()

    def wait(ref, sem):
        pltpu.make_async_copy(ref, ref, sem).wait()

    def along_y(i):
        k = far_first(i, NY)
        return k, device((y + k) % NY, x, z, core)

    def along_z(i):
        k = far_first(i, NZ)
        return k, device(y, x, (z + k) % NZ, core)

    def across(i):
        x2 = (x + far_first(i // NC, NX)) % NX
        c2 = (core + NC - 1 - i % NC) % NC
        return x2 * NC + c2, device(y, x2, z, c2)

    loads = [
        pltpu.make_async_copy(src, dst, load_sem.at[i])
        for i, (src, dst) in enumerate(((q_hbm, q_v), (g_hbm, m_v.at[0]), (e_hbm, m_v.at[1])))
    ]
    for load in loads:
        load.start()

    barrier = pltpu.get_barrier_semaphore()

    def greet(to):
        pl.semaphore_signal(barrier, inc=1, device_id=to, device_id_type=MESH)

    loop(NY - 1, lambda i: greet(along_y(i)[1]))
    loop(NZ - 1, lambda i: greet(along_z(i)[1]))
    loop(NX * NC - 1, lambda i: greet(across(i)[1]))

    for load in loads:
        load.wait()
    q2 = jnp.concatenate(halves(q_v[...]), axis=1)

    def left_rows(i):
        block = span(i * BLOCK, BLOCK, 16)
        both = dot(m_v[0, block, :], q2) + dot(m_v[1, block, :], q2)
        part_v[block, :] = both[:, :rank] + both[:, rank:]

    loop(rows // BLOCK, left_rows)
    pl.semaphore_wait(barrier, NY + NZ + NX * NC - 3)

    mine = x * NC + core

    def scatter(i):
        other, to = across(i)
        send(part_v.at[span(other * chunk, chunk)], a_rx.at[i], a_s.at[i], a_r.at[i], to)

    loop(NX * NC - 1, scatter)

    full = width // 128

    def turn(i):
        at = span(i % full * 128, 128, 128)
        t_v[i // full, at, :] = m_v[i // full, :, at].T

    loop(2 * full, turn)
    if width % 128:

        def turn_rest(i):
            t_v[i, full * 128 :, :] = m_v[i, :, full * 128 :].T

        loop(2, turn_rest)

    def add_chunk(i, total):
        wait(a_rx.at[i], a_r.at[i])
        return total + a_rx[i]

    total = lax.fori_loop(0, NX * NC - 1, add_chunk, part_v[span(mine * chunk, chunk), :])

    def spread_y(ref, s, r):
        def step(i):
            k, to = along_y(i)
            send(ref.at[y], ref.at[y], s.at[k - 1], r.at[k - 1], to)

        return step

    def spread_z(ref, s, r):
        def step(i):
            k, to = along_z(i)
            send(ref.at[z], ref.at[z], s.at[k - 1], r.at[k - 1], to)

        return step

    def collect(ref, r):
        n = ref.shape[0]
        loop(n - 1, lambda i: wait(ref.at[0], r.at[i]))
        value = ref[0]
        for k in range(1, n):
            value = value + ref[k]
        return value

    by_rx[y] = total[:SPLIT]
    bz_rx[z] = total[SPLIT:]
    loop(NY - 1, spread_y(by_rx, by_s, by_r))
    loop(NZ - 1, spread_z(bz_rx, bz_s, bz_r))
    dz_rx[z] = collect(by_rx, by_r)
    loop(NZ - 1, spread_z(dz_rx, dz_s, dz_r))
    dy_rx[y] = collect(bz_rx, bz_r)
    loop(NY - 1, spread_y(dy_rx, dy_s, dy_r))
    mean_v[span(mine * chunk, SPLIT), :] = collect(dz_rx, dz_r) / replicas
    mean_v[span(mine * chunk + SPLIT, chunk - SPLIT), :] = collect(dy_rx, dy_r) / replicas

    own = mean_v.at[span(mine * chunk, chunk)]
    loop(NX * NC - 1, lambda i: send(own, own, c_s.at[i], c_r.at[i], across(i)[1]))
    loop(NX * NC - 1, lambda i: wait(own, c_r.at[i]))

    p2_v[...] = jnp.concatenate(halves(mean_v[...]), axis=1)

    def right_rows(i):
        block = span(i * TALL, TALL, 16)
        both = dot(t_v[0, block, :], p2_v[...]) + dot(t_v[1, block, :], p2_v[...])
        qp_v[block, :] = both[:, :rank] + both[:, rank:]

    loop(width // TALL, right_rows)

    def piece(x, y):
        return span(x * cols + y * PIECE, PIECE)

    def local_piece(y):
        return span(y * PIECE, PIECE)

    def along_x(i):
        k = far_first(i, NX)
        return k - 1, (x + k) % NX, device(y, (x + k) % NX, z, core)

    def scatter_x(i):
        ky = far_first(i, NY)
        y2 = (y + ky) % NY

        @pl.when(y2 < OWNERS)
        def _():
            def step(j):
                kx, x2, to = along_x(j)
                send(qp_v.at[piece(x2, y2)], rx_rx.at[kx, local_piece(y2)], rx_s.at[kx, ky], rx_r.at[kx, ky], to)

            loop(NX - 1, step)

    loop(NY, scatter_x)

    mean = mean_v[...]
    c_v[...] = dot(mean, mean, ((0,), (0,)), lax.Precision.HIGHEST)

    def scatter_y(i):
        ky = far_first(i, NY)
        y2 = (y + ky) % NY

        @pl.when(y2 < OWNERS)
        def _():
            value = qp_v[piece(x, y2), :]
            for kx in range(NX - 1):
                wait(rx_rx.at[kx, local_piece(y2)], rx_r.at[kx, ky])
                value = value + rx_rx[kx, local_piece(y2), :]
            ry_v[local_piece(y2), :] = value

            @pl.when(ky > 0)
            def _():
                send(ry_v.at[local_piece(y2)], ry_rx.at[ky - 1], ry_s.at[ky - 1], ry_r.at[ky - 1], along_y(i)[1])

    def own_piece():
        def add(i, value):
            wait(ry_rx.at[i], ry_r.at[i])
            return value + ry_rx[i]

        right_v[piece(x, y), :] = lax.fori_loop(0, NY - 1, add, ry_v[local_piece(y), :]) / replicas
        out = right_v.at[piece(x, y)]

        def to_y(i):
            k, to = along_y(i)
            send(out, out, gy_s.at[k - 1], gy_r.at[k - 1], to)

        def to_x(j):
            kx, _, to = along_x(j)
            send(out, out, gx_s.at[kx, 0], gx_r.at[kx, 0], to)

        loop(NY - 1, to_y)
        loop(NX - 1, to_x)

    def gather(i):
        ky = far_first(NY - 2 - i, NY)
        y2 = (y + NY - ky) % NY

        @pl.when(y2 < OWNERS)
        def _():
            got = right_v.at[piece(x, y2)]
            wait(got, gy_r.at[ky - 1])

            def step(j):
                kx, _, to = along_x(j)
                send(got, got, gx_s.at[kx, ky], gx_r.at[kx, ky], to)

            loop(NX - 1, step)

    steps = rank // 8
    cut1, cut2 = steps // 4, steps * 5 // 8

    def stage(s):
        first = jnp.where(s == 0, 0, jnp.where(s == 1, cut1, cut2))
        last = jnp.where(s == 0, cut1, jnp.where(s == 1, cut2, steps))
        c_v[...] = lax.fori_loop(first, last, panel, c_v[...])

        @pl.when(s == 0)
        def _():
            loop(NY, scatter_y)

        @pl.when((s == 1) & (y < OWNERS))
        def _():
            own_piece()

        @pl.when(s == 2)
        def _():
            loop(NY - 1, gather)

    loop(3, stage)

    inverse = inverse_factor(c_v[...])
    inverse_out[...] = inverse
    p_hat_out[...] = dot(mean_v[...], inverse, ((1,), (1,)), lax.Precision.HIGHEST)

    def done_across(i):
        wait(own, a_s.at[i])
        wait(own, c_s.at[i])

    def done_y(i):
        wait(by_rx.at[0], by_s.at[i])
        wait(dy_rx.at[0], dy_s.at[i])

    def done_z(i):
        wait(bz_rx.at[0], bz_s.at[i])
        wait(dz_rx.at[0], dz_s.at[i])

    loop(NX * NC - 1, done_across)
    loop(NY - 1, done_y)
    loop(NZ - 1, done_z)
    one = right_v.at[span(0, PIECE)]

    def done_pieces(ky):
        @pl.when((y + ky) % NY < OWNERS)
        def _():
            loop(NX - 1, lambda kx: wait(one, rx_s.at[kx, ky]))

            @pl.when(ky > 0)
            def _():
                wait(one, ry_s.at[ky - 1])

        @pl.when((y + NY - ky) % NY < OWNERS)
        def _():
            def step(kx):
                wait(one, gx_r.at[kx, ky])
                wait(one, gx_s.at[kx, ky])

            loop(NX - 1, step)

        @pl.when((ky > 0) & (y < OWNERS))
        def _():
            wait(one, gy_s.at[ky - 1])

    loop(NY, done_pieces)
    right_out[...] = right_v[...]


def finish(
    g_hbm, e_hbm, right_v, p_hat_v, inverse_v, approx_hbm, q_hbm, error_hbm,
    m_v, q_v, q3_v, approx_v, error_v, load_sem, q_sem, sems,
):
    _, rows, width = m_v.shape
    loads = [pltpu.make_async_copy(src, m_v.at[i], load_sem.at[i]) for i, src in enumerate((g_hbm, e_hbm))]
    for load in loads:
        load.start()
    inverse_high, inverse_low = halves(inverse_v[...])
    inverse3 = jnp.concatenate([inverse_high, inverse_high, inverse_low], axis=1)

    def right_rows(i):
        block = span(i * TALL, TALL, 16)
        high, low = halves(right_v[block, :])
        q_next = dot(jnp.concatenate([high, low, high], axis=1), inverse3, ((1,), (1,)))
        q_v[block, :] = q_next
        high, low = halves(q_next)
        q3_v[block, :] = jnp.concatenate([high, high, low], axis=1)

    loop(width // TALL, right_rows)
    q_copy = pltpu.make_async_copy(q_v, q_hbm, q_sem)
    q_copy.start()
    for load in loads:
        load.wait()

    def left_rows(i):
        block = span(i * BLOCK, BLOCK, 16)
        high, low = halves(p_hat_v[block, :])
        full = dot(jnp.concatenate([high, low, high], axis=1), q3_v[...], ((1,), (1,)))
        approx_v[block, :] = full.astype(BF16)
        error_v[block, :] = (m_v[0, block, :].astype(F32) + m_v[1, block, :].astype(F32) - full).astype(BF16)
        pltpu.make_async_copy(approx_v.at[block], approx_hbm.at[block], sems.at[0, i]).start()
        pltpu.make_async_copy(error_v.at[block], error_hbm.at[block], sems.at[1, i]).start()

    def done(i):
        block = span(i * BLOCK, BLOCK, 16)
        pltpu.make_async_copy(approx_v.at[block], approx_hbm.at[block], sems.at[0, i]).wait()
        pltpu.make_async_copy(error_v.at[block], error_hbm.at[block], sems.at[1, i]).wait()

    loop(rows // BLOCK, left_rows)
    loop(rows // BLOCK, done)
    q_copy.wait()


def local(grads, errors, q_start):
    grads, errors = grads[0], errors[0]
    rows, width = grads.shape
    rank = q_start.shape[1]
    chunk = rows // (NX * NC)
    cols = width // NX
    nxc = NX * NC - 1
    anywhere = pl.BlockSpec(memory_space=pl.ANY)
    vmem = pl.BlockSpec(memory_space=pltpu.VMEM)
    dma = pltpu.SemaphoreType.DMA
    right, p_hat, inverse = pl.pallas_call(
        exchange,
        out_shape=(
            jax.ShapeDtypeStruct((width, rank), F32),
            jax.ShapeDtypeStruct((rows, rank), F32),
            jax.ShapeDtypeStruct((rank, rank), F32),
        ),
        in_specs=[anywhere] * 3,
        out_specs=(vmem,) * 3,
        scratch_shapes=[
            pltpu.VMEM((2, rows, width), BF16),
            pltpu.VMEM((width, rank), F32),
            pltpu.VMEM((2, width, rows), BF16),
            pltpu.VMEM((rows, rank), F32),
            pltpu.VMEM((nxc, chunk, rank), F32),
            pltpu.VMEM((NY, SPLIT, rank), F32),
            pltpu.VMEM((NZ, chunk - SPLIT, rank), F32),
            pltpu.VMEM((NZ, SPLIT, rank), F32),
            pltpu.VMEM((NY, chunk - SPLIT, rank), F32),
            pltpu.VMEM((rows, rank), F32),
            pltpu.VMEM((rows, 2 * rank), BF16),
            pltpu.VMEM((width, rank), F32),
            pltpu.VMEM((NX - 1, cols, rank), F32),
            pltpu.VMEM((cols, rank), F32),
            pltpu.VMEM((NY - 1, PIECE, rank), F32),
            pltpu.VMEM((width, rank), F32),
            pltpu.VMEM((rank, rank), F32),
            dma((3,)),
            dma((nxc,)), dma((nxc,)),
            dma((NY - 1,)), dma((NY - 1,)),
            dma((NZ - 1,)), dma((NZ - 1,)),
            dma((NZ - 1,)), dma((NZ - 1,)),
            dma((NY - 1,)), dma((NY - 1,)),
            dma((nxc,)), dma((nxc,)),
            dma((NX - 1, NY)), dma((NX - 1, NY)),
            dma((NY - 1,)), dma((NY - 1,)),
            dma((NY - 1,)), dma((NY - 1,)),
            dma((NX - 1, NY)), dma((NX - 1, NY)),
        ],
        compiler_params=pltpu.CompilerParams(collective_id=0, has_side_effects=True, vmem_limit_bytes=LIMIT),
        name="exchange",
    )(grads, errors, q_start)

    approx, q_next, error_next = pl.pallas_call(
        finish,
        out_shape=(
            jax.ShapeDtypeStruct((rows, width), BF16),
            jax.ShapeDtypeStruct((width, rank), F32),
            jax.ShapeDtypeStruct((rows, width), BF16),
        ),
        in_specs=[anywhere] * 2 + [vmem] * 3,
        out_specs=(anywhere,) * 3,
        scratch_shapes=[
            pltpu.VMEM((2, rows, width), BF16),
            pltpu.VMEM((width, rank), F32),
            pltpu.VMEM((width, 3 * rank), BF16),
            pltpu.VMEM((rows, width), BF16),
            pltpu.VMEM((rows, width), BF16),
            dma((2,)),
            dma,
            dma((2, rows // BLOCK)),
        ],
        compiler_params=pltpu.CompilerParams(vmem_limit_bytes=LIMIT),
        name="finish",
    )(grads, errors, right, p_hat, inverse)
    return approx, q_next, error_next[None]


def solution(mesh):
    return jax.shard_map(
        local,
        mesh=mesh,
        in_specs=(P("dp", None, "mp"), P("dp", None, "mp"), P("mp", None)),
        out_specs=(P(None, "mp"), P("mp", None), P("dp", None, "mp")),
        check_vma=False,
    )
```

```python
import functools

import jax
import jax.numpy as jnp
from jax import lax
from jax.experimental import pallas as pl
from jax.experimental.pallas import tpu as pltpu
from jax.sharding import PartitionSpec as P

MESH = pl.DeviceIdType.MESH
F32 = jnp.float32
BF16 = jnp.bfloat16

NX, NY, NZ, NC = 4, 8, 8, 2
OWNERS = 7
PIECE = 40
SPLIT = 32
BLOCK = 112
TALL = 224
FIRST = 3
LIMIT = 53 * 2**20


def loop(n, body):
    def step(i, carry):
        body(i)
        return carry

    lax.fori_loop(0, n, step, 0)


def far_first(i, n):
    return n // 2 + (i + 1) // 2 * (1 - 2 * (i % 2))


def dot(a, b, dims=((1,), (0,)), precision=None):
    return lax.dot_general(a, b, (dims, ((), ())), precision=precision, preferred_element_type=F32)


def halves(a):
    high = a.astype(BF16)
    return high, (a - high.astype(F32)).astype(BF16)


def span(start, size, unit=8):
    return pl.ds(pl.multiple_of(start, unit), size)


def panel(index, c):
    n = c.shape[0]
    lanes = lax.broadcasted_iota(jnp.int32, (1, n), 1)
    rows = lax.broadcasted_iota(jnp.int32, (n, 1), 0)
    active = rows < n - 8 * index
    live = jnp.where(active, c, 0.0)
    top = c[:8, :]

    def copies(row):
        return jnp.broadcast_to(row, (8, n))

    heads = [jnp.broadcast_to(top[:, k : k + 1], (8, n)) for k in range(8)]
    columns = [jnp.broadcast_to(live[8:, k : k + 1], (n - 8, n)) for k in range(8)]
    left = {(i, k): copies(heads[k][i : i + 1, :]) for k in range(8) for i in range(k, 8)}
    lower, scale = {}, []
    for j in range(8):
        scale.append(lax.rsqrt(left[j, j]))
        for i in range(j + 1, 8):
            lower[i, j] = left[i, j] * scale[j]
        for k in range(j + 1, 8):
            for i in range(k, 8):
                left[i, k] = left[i, k] - lower[i, j] * lower[k, j]
    done = []
    for j in range(8):
        value = copies(jnp.where(lanes < 8, jnp.where(lanes == j, 1.0, 0.0), top[j : j + 1, :]))
        for k in range(j):
            value = value - lower[j, k] * done[k]
        done.append(value * scale[j])
    solved = [None] * 8
    for k in reversed(range(8)):
        value = done[k]
        for j in range(k + 1, 8):
            value = value - lower[j, k] * solved[j]
        solved[k] = value * scale[k]
    rest = jnp.where(active[8:] & (lanes < 8), 0.0, c[8:])
    for k in range(8):
        rest = rest - columns[k] * solved[k][:1]
    top = jnp.concatenate([row[:1] for row in done], axis=0)
    return jnp.concatenate([pltpu.roll(rest, n - 8, 1), pltpu.roll(top, n - 8, 1)], axis=0)


def inverse_factor(c):
    n = c.shape[0]
    rows = lax.broadcasted_iota(jnp.int32, (n, n), 0)
    lanes = lax.broadcasted_iota(jnp.int32, (n, n), 1)
    return jnp.where(lanes <= rows, c, 0.0)


def times_transposed(a, b):
    a_high, a_low = halves(a)
    b_high, b_low = halves(b)
    return dot(
        jnp.concatenate([a_high, a_low, a_high], axis=1), jnp.concatenate([b_high, b_high, b_low], axis=1), ((1,), (1,))
    )


def exchange(
    g_hbm, e_hbm, q_hbm, right_out, p_hat_out,
    m_v, q_v, t_v, part_v, a_rx, by_rx, bz_rx, dz_rx, dy_rx, mean_v, p2_v,
    qp_v, rx_rx, ry_v, ry_rx, right_v, c_v,
    load_sem, a_s, a_r, by_s, by_r, bz_s, bz_r, dz_s, dz_r, dy_s, dy_r, c_s, c_r,
    rx_s, rx_r, ry_s, ry_r, gy_s, gy_r, gx_s, gx_r,
):
    _, rows, width = m_v.shape
    rank = q_v.shape[1]
    chunk = rows // (NX * NC)
    cols = width // NX
    replicas = NX * NY
    nxc = NX * NC
    dp = lax.axis_index("dp")
    mp = lax.axis_index("mp")
    y, x, z, core = dp // NX, dp % NX, mp // NC, mp % NC

    def device(y, x, z, core):
        return (y * NX + x, z * NC + core)

    def send(src, dst, s, r, to):
        pltpu.make_async_remote_copy(
            src_ref=src, dst_ref=dst, send_sem=s, recv_sem=r, device_id=to, device_id_type=MESH
        ).start()

    def wait(ref, sem):
        pltpu.make_async_copy(ref, ref, sem).wait()

    def along_y(i):
        k = far_first(i, NY)
        return k, device((y + k) % NY, x, z, core)

    def along_z(i):
        k = far_first(i, NZ)
        return k, device(y, x, (z + k) % NZ, core)

    def across(i):
        x2 = (x + far_first(i // NC, NX)) % NX
        c2 = (core + NC - 1 - i % NC) % NC
        return x2 * NC + c2, device(y, x2, z, c2)

    loads = [
        pltpu.make_async_copy(src, dst, load_sem.at[i])
        for i, (src, dst) in enumerate(((q_hbm, q_v), (g_hbm, m_v.at[0]), (e_hbm, m_v.at[1])))
    ]
    for load in loads:
        load.start()

    barrier = pltpu.get_barrier_semaphore()

    def greet(to):
        pl.semaphore_signal(barrier, inc=1, device_id=to, device_id_type=MESH)

    loop(max(NY, NZ) - 1, lambda i: (greet(along_y(i)[1]), greet(along_z(i)[1])))
    loop(nxc - 1, lambda i: greet(across(i)[1]))

    for load in loads:
        load.wait()
    q2 = jnp.concatenate(halves(q_v[...]), axis=1)

    def left_rows(i):
        block = span(i * BLOCK, BLOCK, 16)
        both = dot(m_v[0, block, :], q2) + dot(m_v[1, block, :], q2)
        part_v[block, :] = both[:, :rank] + both[:, rank:]

    loop(rows // BLOCK, left_rows)

    pl.semaphore_wait(barrier, NY + NZ + nxc - 3)

    mine = x * NC + core

    def scatter(i):
        other, to = across(i)
        send(part_v.at[span(other * chunk, chunk)], a_rx.at[i], a_s, a_r.at[i], to)

    loop(nxc - 1, scatter)

    full = width // 128

    def turn(i):
        at = span(i % full * 128, 128, 128)
        t_v[i // full, at, :] = m_v[i // full, :, at].T

    loop(2 * full, turn)
    if width % 128:

        def turn_rest(i):
            t_v[i, full * 128 :, :] = m_v[i, :, full * 128 :].T

        loop(2, turn_rest)

    def add_chunk(i, total):
        wait(a_rx.at[i], a_r.at[i])
        return total + a_rx[i]

    total = lax.fori_loop(0, nxc - 1, add_chunk, part_v[span(mine * chunk, chunk), :])

    def spread_y(ref, s, r, i):
        send(ref.at[y], ref.at[y], s, r, along_y(i)[1])

    def spread_z(ref, s, r, i):
        send(ref.at[z], ref.at[z], s, r, along_z(i)[1])

    def collect(ref, r):
        n = ref.shape[0]
        wait(ref.at[: n - 1], r)
        value = ref[0]
        for k in range(1, n):
            value = value + ref[k]
        return value

    by_rx[y] = total[:SPLIT]
    bz_rx[z] = total[SPLIT:]

    def spread(i):
        spread_y(by_rx, by_s, by_r, i)
        spread_z(bz_rx, bz_s, bz_r, i)

    loop(max(NY, NZ) - 1, spread)
    dz_rx[z] = collect(by_rx, by_r)
    loop(NZ - 1, functools.partial(spread_z, dz_rx, dz_s, dz_r))
    dy_rx[y] = collect(bz_rx, bz_r)
    loop(NY - 1, functools.partial(spread_y, dy_rx, dy_s, dy_r))
    mean_v[span(mine * chunk, SPLIT), :] = collect(dz_rx, dz_r) / replicas
    mean_v[span(mine * chunk + SPLIT, chunk - SPLIT), :] = collect(dy_rx, dy_r) / replicas

    own = mean_v.at[span(mine * chunk, chunk)]
    loop(nxc - 1, lambda i: send(own, own, c_s, c_r, across(i)[1]))

    wait(part_v.at[pl.ds(0, (nxc - 1) * chunk)], a_s)
    wait(by_rx.at[: NY - 1], by_s)
    wait(bz_rx.at[: NZ - 1], bz_s)
    wait(dz_rx.at[: NZ - 1], dz_s)
    wait(dy_rx.at[: NY - 1], dy_s)
    wait(mean_v.at[pl.ds(0, (nxc - 1) * chunk)], c_r)
    wait(mean_v.at[pl.ds(0, (nxc - 1) * chunk)], c_s)
    p2_v[...] = jnp.concatenate(halves(mean_v[...]), axis=1)

    def right_rows(i):
        block = span(i * TALL, TALL, 16)
        both = dot(t_v[0, block, :], p2_v[...]) + dot(t_v[1, block, :], p2_v[...])
        qp_v[block, :] = both[:, :rank] + both[:, rank:]

    loop(width // TALL, right_rows)

    def piece(x, y):
        return span(x * cols + y * PIECE, PIECE)

    def local_piece(y):
        return span(y * PIECE, PIECE)

    def along_x(i):
        k = far_first(i, NX)
        return k - 1, (x + k) % NX, device(y, (x + k) % NX, z, core)

    def scatter_x(i):
        ky = far_first(i, NY)
        y2 = (y + ky) % NY

        @pl.when(y2 < OWNERS)
        def _():
            def step(j):
                kx, x2, to = along_x(j)
                send(qp_v.at[piece(x2, y2)], rx_rx.at[kx, local_piece(y2)], rx_s, rx_r.at[kx, ky], to)

            loop(NX - 1, step)

    loop(NY, scatter_x)
    mean = mean_v[...]
    c_v[...] = dot(mean, mean, ((0,), (0,)), lax.Precision.HIGHEST)

    def scatter_y(i):
        ky = far_first(i, NY)
        y2 = (y + ky) % NY

        @pl.when(y2 < OWNERS)
        def _():
            value = qp_v[piece(x, y2), :]
            for kx in range(NX - 1):
                wait(rx_rx.at[kx, local_piece(y2)], rx_r.at[kx, ky])
                value = value + rx_rx[kx, local_piece(y2), :]
            ry_v[local_piece(y2), :] = value

            @pl.when(ky > 0)
            def _():
                send(ry_v.at[local_piece(y2)], ry_rx.at[ky - 1], ry_s, ry_r.at[ky - 1], along_y(i)[1])

    steps = rank // 8

    def stage(i):
        first = jnp.where(i == 0, 0, FIRST + i - 1)
        last = jnp.where(i == NY, steps, FIRST + i)
        c_v[...] = lax.fori_loop(first, last, panel, c_v[...])

        @pl.when(i < NY)
        def _():
            scatter_y(i)

    loop(NY + 1, stage)
    inverse = inverse_factor(c_v[...])

    def to_x(ref):
        loop(NX - 1, lambda j: send(ref, ref, gx_s, gx_r, along_x(j)[2]))

    @pl.when(y < OWNERS)
    def _():
        def add(i, value):
            wait(ry_rx.at[i], ry_r.at[i])
            return value + ry_rx[i]

        total = lax.fori_loop(0, NY - 1, add, ry_v[local_piece(y), :])
        right_v[piece(x, y), :] = times_transposed(total, inverse) / replicas
        out = right_v.at[piece(x, y)]
        loop(NY - 1, lambda i: send(out, out, gy_s, gy_r.at[along_y(i)[0] - 1], along_y(i)[1]))
        to_x(out)

    p_hat_out[...] = times_transposed(mean_v[...], inverse)
    sent = qp_v.at[pl.ds(0, (NX - 1) * OWNERS * PIECE)]
    wait(sent, rx_s)

    wait(ry_v.at[pl.ds(0, (OWNERS - 1) * PIECE)], ry_s)

    @pl.when(y >= OWNERS)
    def _():
        wait(ry_v.at[pl.ds(0, PIECE)], ry_s)

    def pass_on(i):
        ky = far_first(NY - 2 - i, NY)
        y2 = (y + NY - ky) % NY

        @pl.when(y2 < OWNERS)
        def _():
            got = right_v.at[piece(x, y2)]
            wait(got, gy_r.at[ky - 1])
            to_x(got)

    loop(NY - 1, pass_on)

    @pl.when(y < OWNERS)
    def _():
        wait(qp_v.at[pl.ds(0, (NY - 1) * PIECE)], gy_s)

    wait(sent, gx_r)
    wait(sent, gx_s)
    right_out[...] = right_v[...]


def finish(
    g_hbm, e_hbm, q_v, p_hat_v, approx_hbm, q_hbm, error_hbm,
    m_v, q3_v, approx_v, error_v, load_sems, q_sem, sems,
):
    _, rows, width = m_v.shape

    def load(i):
        block = span(i * BLOCK, BLOCK, 16)
        return [
            pltpu.make_async_copy(src.at[block], m_v.at[k, block], load_sems.at[k, i])
            for k, src in enumerate((g_hbm, e_hbm))
        ]

    loop(rows // BLOCK, lambda i: [copy.start() for copy in load(i)])
    q_copy = pltpu.make_async_copy(q_v, q_hbm, q_sem)
    q_copy.start()

    def right_rows(i):
        block = span(i * TALL, TALL, 16)
        high, low = halves(q_v[block, :])
        q3_v[block, :] = jnp.concatenate([high, high, low], axis=1)

    loop(width // TALL, right_rows)

    def stores(i):
        block = span(i * BLOCK, BLOCK, 16)
        return [
            pltpu.make_async_copy(src.at[block], dst.at[block], sems.at[k, i])
            for k, (src, dst) in enumerate(((approx_v, approx_hbm), (error_v, error_hbm)))
        ]

    def left_rows(i):
        block = span(i * BLOCK, BLOCK, 16)
        high, low = halves(p_hat_v[block, :])
        full = dot(jnp.concatenate([high, low, high], axis=1), q3_v[...], ((1,), (1,)))
        approx_v[block, :] = full.astype(BF16)
        for copy in load(i):
            copy.wait()
        error_v[block, :] = (m_v[0, block, :].astype(F32) + m_v[1, block, :].astype(F32) - full).astype(BF16)
        for copy in stores(i):
            copy.start()

    loop(rows // BLOCK, left_rows)
    loop(rows // BLOCK, lambda i: [copy.wait() for copy in stores(i)])
    q_copy.wait()


def local(grads, errors, q_start):
    grads, errors = grads[0], errors[0]
    rows, width = grads.shape
    rank = q_start.shape[1]
    chunk = rows // (NX * NC)
    cols = width // NX
    nxc = NX * NC - 1
    anywhere = pl.BlockSpec(memory_space=pl.ANY)
    vmem = pl.BlockSpec(memory_space=pltpu.VMEM)
    dma = pltpu.SemaphoreType.DMA
    right, p_hat = pl.pallas_call(
        exchange,
        out_shape=(
            jax.ShapeDtypeStruct((width, rank), F32),
            jax.ShapeDtypeStruct((rows, rank), F32),
        ),
        in_specs=[anywhere] * 3,
        out_specs=(vmem,) * 2,
        scratch_shapes=[
            pltpu.VMEM((2, rows, width), BF16),
            pltpu.VMEM((width, rank), F32),
            pltpu.VMEM((2, width, rows), BF16),
            pltpu.VMEM((rows, rank), F32),
            pltpu.VMEM((nxc, chunk, rank), F32),
            pltpu.VMEM((NY, SPLIT, rank), F32),
            pltpu.VMEM((NZ, chunk - SPLIT, rank), F32),
            pltpu.VMEM((NZ, SPLIT, rank), F32),
            pltpu.VMEM((NY, chunk - SPLIT, rank), F32),
            pltpu.VMEM((rows, rank), F32),
            pltpu.VMEM((rows, 2 * rank), BF16),
            pltpu.VMEM((width, rank), F32),
            pltpu.VMEM((NX - 1, cols, rank), F32),
            pltpu.VMEM((cols, rank), F32),
            pltpu.VMEM((NY - 1, PIECE, rank), F32),
            pltpu.VMEM((width, rank), F32),
            pltpu.VMEM((rank, rank), F32),
            dma((3,)),
            dma, dma((nxc,)),
            dma, dma, dma, dma, dma, dma, dma, dma,
            dma, dma,
            dma, dma((NX - 1, NY)),
            dma, dma((NY - 1,)),
            dma, dma((NY - 1,)),
            dma, dma,
        ],
        compiler_params=pltpu.CompilerParams(collective_id=0, has_side_effects=True, vmem_limit_bytes=LIMIT),
        name="exchange",
    )(grads, errors, q_start)

    approx, q_next, error_next = pl.pallas_call(
        finish,
        out_shape=(
            jax.ShapeDtypeStruct((rows, width), BF16),
            jax.ShapeDtypeStruct((width, rank), F32),
            jax.ShapeDtypeStruct((rows, width), BF16),
        ),
        in_specs=[anywhere] * 2 + [vmem] * 2,
        out_specs=(anywhere,) * 3,
        scratch_shapes=[
            pltpu.VMEM((2, rows, width), BF16),
            pltpu.VMEM((width, 3 * rank), BF16),
            pltpu.VMEM((rows, width), BF16),
            pltpu.VMEM((rows, width), BF16),
            dma((2, rows // BLOCK)),
            dma,
            dma((2, rows // BLOCK)),
        ],
        compiler_params=pltpu.CompilerParams(vmem_limit_bytes=LIMIT),
        name="finish",
    )(grads, errors, right, p_hat)
    return approx, q_next, error_next[None]


def solution(mesh):
    return jax.shard_map(
        local,
        mesh=mesh,
        in_specs=(P("dp", None, "mp"), P("dp", None, "mp"), P("mp", None)),
        out_specs=(P(None, "mp"), P("mp", None), P("dp", None, "mp")),
        check_vma=False,
    )
```

```python
import functools

import jax
import jax.numpy as jnp
from jax import lax
from jax.experimental import pallas as pl
from jax.experimental.pallas import tpu as pltpu
from jax.sharding import PartitionSpec as P

MESH = pl.DeviceIdType.MESH
F32 = jnp.float32
BF16 = jnp.bfloat16

NX, NY, NZ, NC = 4, 8, 8, 2
OWNERS = 7
PIECE = 40
SPLIT = 32
BLOCK = 112
TALL = 224
FIRST = 3
LIMIT = 51 * 2**20


def loop(n, body):
    def step(i, carry):
        body(i)
        return carry

    lax.fori_loop(0, n, step, 0)


def far_first(i, n):
    return n // 2 + (i + 1) // 2 * (1 - 2 * (i % 2))


def dot(a, b, dims=((1,), (0,)), precision=None):
    return lax.dot_general(a, b, (dims, ((), ())), precision=precision, preferred_element_type=F32)


def halves(a):
    high = a.astype(BF16)
    return high, (a - high.astype(F32)).astype(BF16)


def span(start, size, unit=8):
    return pl.ds(pl.multiple_of(start, unit), size)


def panel(index, c):
    n = c.shape[0]
    lanes = lax.broadcasted_iota(jnp.int32, (1, n), 1)
    rows = lax.broadcasted_iota(jnp.int32, (n, 1), 0)
    active = rows < n - 8 * index
    live = jnp.where(active, c, 0.0)
    top = c[:8, :]

    def copies(row):
        return jnp.broadcast_to(row, (8, n))

    heads = [jnp.broadcast_to(top[:, k : k + 1], (8, n)) for k in range(8)]
    columns = [jnp.broadcast_to(live[8:, k : k + 1], (n - 8, n)) for k in range(8)]
    left = {(i, k): copies(heads[k][i : i + 1, :]) for k in range(8) for i in range(k, 8)}
    lower, scale = {}, []
    for j in range(8):
        scale.append(lax.rsqrt(left[j, j]))
        for i in range(j + 1, 8):
            lower[i, j] = left[i, j] * scale[j]
        for k in range(j + 1, 8):
            for i in range(k, 8):
                left[i, k] = left[i, k] - lower[i, j] * lower[k, j]
    done = []
    for j in range(8):
        value = copies(jnp.where(lanes < 8, jnp.where(lanes == j, 1.0, 0.0), top[j : j + 1, :]))
        for k in range(j):
            value = value - lower[j, k] * done[k]
        done.append(value * scale[j])
    solved = [None] * 8
    for k in reversed(range(8)):
        value = done[k]
        for j in range(k + 1, 8):
            value = value - lower[j, k] * solved[j]
        solved[k] = value * scale[k]
    rest = jnp.where(active[8:] & (lanes < 8), 0.0, c[8:])
    for k in range(8):
        rest = rest - columns[k] * solved[k][:1]
    top = jnp.concatenate([row[:1] for row in done], axis=0)
    return jnp.concatenate([pltpu.roll(rest, n - 8, 1), pltpu.roll(top, n - 8, 1)], axis=0)


def inverse_factor(c):
    n = c.shape[0]
    rows = lax.broadcasted_iota(jnp.int32, (n, n), 0)
    lanes = lax.broadcasted_iota(jnp.int32, (n, n), 1)
    return jnp.where(lanes <= rows, c, 0.0)


def times_transposed(a, b):
    a_high, a_low = halves(a)
    b_high, b_low = halves(b)
    return dot(
        jnp.concatenate([a_high, a_low, a_high], axis=1), jnp.concatenate([b_high, b_high, b_low], axis=1), ((1,), (1,))
    )


def exchange(
    g_hbm, e_hbm, q_hbm, m_v, right_out, p_hat_out,
    q_v, t_v, part_v, a_rx, by_rx, bz_rx, dz_rx, dy_rx, mean_v, p2_v,
    qp_v, rx_rx, ry_v, ry_rx, right_v, c_v,
    q_sem, load_sem, a_s, a_r, by_s, by_r, bz_s, bz_r, dz_s, dz_r, dy_s, dy_r, c_s, c_r,
    rx_s, rx_r, ry_s, ry_r, gy_s, gy_r, gx_s, gx_r,
):
    _, rows, width = m_v.shape
    rank = q_v.shape[1]
    chunk = rows // (NX * NC)
    cols = width // NX
    replicas = NX * NY
    nxc = NX * NC
    dp = lax.axis_index("dp")
    mp = lax.axis_index("mp")
    y, x, z, core = dp // NX, dp % NX, mp // NC, mp % NC

    def device(y, x, z, core):
        return (y * NX + x, z * NC + core)

    def send(src, dst, s, r, to):
        pltpu.make_async_remote_copy(
            src_ref=src, dst_ref=dst, send_sem=s, recv_sem=r, device_id=to, device_id_type=MESH
        ).start()

    def wait(ref, sem):
        pltpu.make_async_copy(ref, ref, sem).wait()

    def along_y(i):
        k = far_first(i, NY)
        return k, device((y + k) % NY, x, z, core)

    def along_z(i):
        k = far_first(i, NZ)
        return k, device(y, x, (z + k) % NZ, core)

    def across(i):
        x2 = (x + far_first(i // NC, NX)) % NX
        c2 = (core + NC - 1 - i % NC) % NC
        return x2 * NC + c2, device(y, x2, z, c2)

    def load(i):
        block = span(i * BLOCK, BLOCK, 16)
        return [
            pltpu.make_async_copy(src.at[block], m_v.at[k, block], load_sem.at[k, i])
            for k, src in enumerate((g_hbm, e_hbm))
        ]

    q_load = pltpu.make_async_copy(q_hbm, q_v, q_sem)
    q_load.start()
    loop(rows // BLOCK, lambda i: [copy.start() for copy in load(i)])

    barrier = pltpu.get_barrier_semaphore()

    def greet(to):
        pl.semaphore_signal(barrier, inc=1, device_id=to, device_id_type=MESH)

    loop(max(NY, NZ) - 1, lambda i: (greet(along_y(i)[1]), greet(along_z(i)[1])))
    loop(nxc - 1, lambda i: greet(across(i)[1]))

    q_load.wait()
    q2 = jnp.concatenate(halves(q_v[...]), axis=1)

    def left_rows(i):
        block = span(i * BLOCK, BLOCK, 16)
        for copy in load(i):
            copy.wait()
        both = dot(m_v[0, block, :], q2) + dot(m_v[1, block, :], q2)
        part_v[block, :] = both[:, :rank] + both[:, rank:]

    loop(rows // BLOCK, left_rows)

    pl.semaphore_wait(barrier, NY + NZ + nxc - 3)

    mine = x * NC + core

    def scatter(i):
        other, to = across(i)
        send(part_v.at[span(other * chunk, chunk)], a_rx.at[i], a_s, a_r.at[i], to)

    loop(nxc - 1, scatter)

    full = width // 128

    def turn(i):
        at = span(i % full * 128, 128, 128)
        t_v[i // full, at, :] = m_v[i // full, :, at].T

    loop(2 * full, turn)
    if width % 128:

        def turn_rest(i):
            t_v[i, full * 128 :, :] = m_v[i, :, full * 128 :].T

        loop(2, turn_rest)

    def add_chunk(i, total):
        wait(a_rx.at[i], a_r.at[i])
        return total + a_rx[i]

    total = lax.fori_loop(0, nxc - 1, add_chunk, part_v[span(mine * chunk, chunk), :])

    def spread_y(ref, s, r, i):
        send(ref.at[y], ref.at[y], s, r, along_y(i)[1])

    def spread_z(ref, s, r, i):
        send(ref.at[z], ref.at[z], s, r, along_z(i)[1])

    def collect(ref, r):
        n = ref.shape[0]
        wait(ref.at[: n - 1], r)
        value = ref[0]
        for k in range(1, n):
            value = value + ref[k]
        return value

    by_rx[y] = total[:SPLIT]
    bz_rx[z] = total[SPLIT:]

    def spread(i):
        spread_y(by_rx, by_s, by_r, i)
        spread_z(bz_rx, bz_s, bz_r, i)

    loop(max(NY, NZ) - 1, spread)
    dz_rx[z] = collect(by_rx, by_r)
    loop(NZ - 1, functools.partial(spread_z, dz_rx, dz_s, dz_r))
    dy_rx[y] = collect(bz_rx, bz_r)
    loop(NY - 1, functools.partial(spread_y, dy_rx, dy_s, dy_r))
    mean_v[span(mine * chunk, SPLIT), :] = collect(dz_rx, dz_r) / replicas
    mean_v[span(mine * chunk + SPLIT, chunk - SPLIT), :] = collect(dy_rx, dy_r) / replicas

    own = mean_v.at[span(mine * chunk, chunk)]
    loop(nxc - 1, lambda i: send(own, own, c_s, c_r, across(i)[1]))

    wait(part_v.at[pl.ds(0, (nxc - 1) * chunk)], a_s)
    wait(by_rx.at[: NY - 1], by_s)
    wait(bz_rx.at[: NZ - 1], bz_s)
    wait(dz_rx.at[: NZ - 1], dz_s)
    wait(dy_rx.at[: NY - 1], dy_s)
    wait(mean_v.at[pl.ds(0, (nxc - 1) * chunk)], c_r)
    wait(mean_v.at[pl.ds(0, (nxc - 1) * chunk)], c_s)
    p2_v[...] = jnp.concatenate(halves(mean_v[...]), axis=1)

    def right_rows(i):
        block = span(i * TALL, TALL, 16)
        both = dot(t_v[0, block, :], p2_v[...]) + dot(t_v[1, block, :], p2_v[...])
        qp_v[block, :] = both[:, :rank] + both[:, rank:]

    loop(width // TALL, right_rows)

    def piece(x, y):
        return span(x * cols + y * PIECE, PIECE)

    def local_piece(y):
        return span(y * PIECE, PIECE)

    def along_x(i):
        k = far_first(i, NX)
        return k - 1, (x + k) % NX, device(y, (x + k) % NX, z, core)

    def scatter_x(i):
        ky = far_first(i, NY)
        y2 = (y + ky) % NY

        @pl.when(y2 < OWNERS)
        def _():
            def step(j):
                kx, x2, to = along_x(j)
                send(qp_v.at[piece(x2, y2)], rx_rx.at[kx, local_piece(y2)], rx_s, rx_r.at[kx, ky], to)

            loop(NX - 1, step)

    loop(NY, scatter_x)
    mean = mean_v[...]
    c_v[...] = dot(mean, mean, ((0,), (0,)), lax.Precision.HIGHEST)

    def scatter_y(i):
        ky = far_first(i, NY)
        y2 = (y + ky) % NY

        @pl.when(y2 < OWNERS)
        def _():
            value = qp_v[piece(x, y2), :]
            for kx in range(NX - 1):
                wait(rx_rx.at[kx, local_piece(y2)], rx_r.at[kx, ky])
                value = value + rx_rx[kx, local_piece(y2), :]
            ry_v[local_piece(y2), :] = value

            @pl.when(ky > 0)
            def _():
                send(ry_v.at[local_piece(y2)], ry_rx.at[ky - 1], ry_s, ry_r.at[ky - 1], along_y(i)[1])

    steps = rank // 8

    def stage(i):
        first = jnp.where(i == 0, 0, FIRST + i - 1)
        last = jnp.where(i == NY, steps, FIRST + i)
        c_v[...] = lax.fori_loop(first, last, panel, c_v[...])

        @pl.when(i < NY)
        def _():
            scatter_y(i)

    loop(NY + 1, stage)
    inverse = inverse_factor(c_v[...])

    def to_x(ref):
        loop(NX - 1, lambda j: send(ref, ref, gx_s, gx_r, along_x(j)[2]))

    @pl.when(y < OWNERS)
    def _():
        def add(i, value):
            wait(ry_rx.at[i], ry_r.at[i])
            return value + ry_rx[i]

        total = lax.fori_loop(0, NY - 1, add, ry_v[local_piece(y), :])
        right_v[piece(x, y), :] = times_transposed(total, inverse) / replicas
        out = right_v.at[piece(x, y)]
        loop(NY - 1, lambda i: send(out, out, gy_s, gy_r.at[along_y(i)[0] - 1], along_y(i)[1]))
        to_x(out)

    p_hat_out[...] = times_transposed(mean_v[...], inverse)
    sent = qp_v.at[pl.ds(0, (NX - 1) * OWNERS * PIECE)]
    wait(sent, rx_s)

    wait(ry_v.at[pl.ds(0, (OWNERS - 1) * PIECE)], ry_s)

    @pl.when(y >= OWNERS)
    def _():
        wait(ry_v.at[pl.ds(0, PIECE)], ry_s)

    def pass_on(i):
        ky = far_first(NY - 2 - i, NY)
        y2 = (y + NY - ky) % NY

        @pl.when(y2 < OWNERS)
        def _():
            got = right_v.at[piece(x, y2)]
            wait(got, gy_r.at[ky - 1])
            to_x(got)

    loop(NY - 1, pass_on)

    @pl.when(y < OWNERS)
    def _():
        wait(qp_v.at[pl.ds(0, (NY - 1) * PIECE)], gy_s)

    wait(sent, gx_r)
    wait(sent, gx_s)
    right_out[...] = right_v[...]


def finish(
    m_v, q_v, p_hat_v, approx_hbm, q_hbm, error_hbm,
    q3_v, approx_v, error_v, q_sem, sems,
):
    _, rows, width = m_v.shape

    q_copy = pltpu.make_async_copy(q_v, q_hbm, q_sem)
    q_copy.start()

    def right_rows(i):
        block = span(i * TALL, TALL, 16)
        high, low = halves(q_v[block, :])
        q3_v[block, :] = jnp.concatenate([high, high, low], axis=1)

    loop(width // TALL, right_rows)

    def stores(i):
        block = span(i * BLOCK, BLOCK, 16)
        return [
            pltpu.make_async_copy(src.at[block], dst.at[block], sems.at[k, i])
            for k, (src, dst) in enumerate(((approx_v, approx_hbm), (error_v, error_hbm)))
        ]

    def left_rows(i):
        block = span(i * BLOCK, BLOCK, 16)
        high, low = halves(p_hat_v[block, :])
        full = dot(jnp.concatenate([high, low, high], axis=1), q3_v[...], ((1,), (1,)))
        approx_v[block, :] = full.astype(BF16)
        error_v[block, :] = (m_v[0, block, :].astype(F32) + m_v[1, block, :].astype(F32) - full).astype(BF16)
        for copy in stores(i):
            copy.start()

    loop(rows // BLOCK, left_rows)
    loop(rows // BLOCK, lambda i: [copy.wait() for copy in stores(i)])
    q_copy.wait()


def local(grads, errors, q_start):
    grads, errors = grads[0], errors[0]
    rows, width = grads.shape
    rank = q_start.shape[1]
    chunk = rows // (NX * NC)
    cols = width // NX
    nxc = NX * NC - 1
    anywhere = pl.BlockSpec(memory_space=pl.ANY)
    vmem = pl.BlockSpec(memory_space=pltpu.VMEM)
    dma = pltpu.SemaphoreType.DMA
    merged, right, p_hat = pl.pallas_call(
        exchange,
        out_shape=(
            pltpu.VMEM((2, rows, width), BF16),
            pltpu.VMEM((width, rank), F32),
            pltpu.VMEM((rows, rank), F32),
        ),
        in_specs=[anywhere] * 3,
        out_specs=(vmem,) * 3,
        scratch_shapes=[
            pltpu.VMEM((width, rank), F32),
            pltpu.VMEM((2, width, rows), BF16),
            pltpu.VMEM((rows, rank), F32),
            pltpu.VMEM((nxc, chunk, rank), F32),
            pltpu.VMEM((NY, SPLIT, rank), F32),
            pltpu.VMEM((NZ, chunk - SPLIT, rank), F32),
            pltpu.VMEM((NZ, SPLIT, rank), F32),
            pltpu.VMEM((NY, chunk - SPLIT, rank), F32),
            pltpu.VMEM((rows, rank), F32),
            pltpu.VMEM((rows, 2 * rank), BF16),
            pltpu.VMEM((width, rank), F32),
            pltpu.VMEM((NX - 1, cols, rank), F32),
            pltpu.VMEM((cols, rank), F32),
            pltpu.VMEM((NY - 1, PIECE, rank), F32),
            pltpu.VMEM((width, rank), F32),
            pltpu.VMEM((rank, rank), F32),
            dma, dma((2, rows // BLOCK)),
            dma, dma((nxc,)),
            dma, dma, dma, dma, dma, dma, dma, dma,
            dma, dma,
            dma, dma((NX - 1, NY)),
            dma, dma((NY - 1,)),
            dma, dma((NY - 1,)),
            dma, dma,
        ],
        compiler_params=pltpu.CompilerParams(collective_id=0, has_side_effects=True, vmem_limit_bytes=LIMIT),
        name="exchange",
    )(grads, errors, q_start)

    approx, q_next, error_next = pl.pallas_call(
        finish,
        out_shape=(
            jax.ShapeDtypeStruct((rows, width), BF16),
            jax.ShapeDtypeStruct((width, rank), F32),
            jax.ShapeDtypeStruct((rows, width), BF16),
        ),
        in_specs=[vmem] * 3,
        out_specs=(anywhere,) * 3,
        scratch_shapes=[
            pltpu.VMEM((width, 3 * rank), BF16),
            pltpu.VMEM((rows, width), BF16),
            pltpu.VMEM((rows, width), BF16),
            dma,
            dma((2, rows // BLOCK)),
        ],
        compiler_params=pltpu.CompilerParams(vmem_limit_bytes=LIMIT - 2**20),
        name="finish",
    )(merged, right, p_hat)
    return approx, q_next, error_next[None]


def solution(mesh):
    return jax.shard_map(
        local,
        mesh=mesh,
        in_specs=(P("dp", None, "mp"), P("dp", None, "mp"), P("mp", None)),
        out_specs=(P(None, "mp"), P("mp", None), P("dp", None, "mp")),
        check_vma=False,
    )
```

```python
import functools

import jax
import jax.numpy as jnp
from jax import lax
from jax.experimental import pallas as pl
from jax.experimental.pallas import tpu as pltpu
from jax.sharding import PartitionSpec as P

MESH = pl.DeviceIdType.MESH
F32 = jnp.float32
BF16 = jnp.bfloat16

NX, NY, NZ, NC = 4, 8, 8, 2
PIECE, LONG, MORE = 32, 40, 3
SPLIT = 32
BLOCK = 112
TALL = 224
FIRST = 5
LIMIT = 51 * 2**20


def loop(n, body):
    def step(i, carry):
        body(i)
        return carry

    lax.fori_loop(0, n, step, 0)


def far_first(i, n):
    return n // 2 + lax.div(i + 1, 2) * (1 - 2 * lax.rem(i, 2))


def dot(a, b, dims=((1,), (0,)), precision=None):
    return lax.dot_general(a, b, (dims, ((), ())), precision=precision, preferred_element_type=F32)


def halves(a):
    high = a.astype(BF16)
    return high, (a - high.astype(F32)).astype(BF16)


def span(start, size, unit=8):
    return pl.ds(pl.multiple_of(start, unit), size)


def panel(index, c):
    n = c.shape[0]
    lanes = lax.broadcasted_iota(jnp.int32, (1, n), 1)
    rows = lax.broadcasted_iota(jnp.int32, (n, 1), 0)
    active = rows < n - 8 * index
    live = jnp.where(active, c, 0.0)
    top = c[:8, :]

    def copies(row):
        return jnp.broadcast_to(row, (8, n))

    heads = [jnp.broadcast_to(top[:, k : k + 1], (8, n)) for k in range(8)]
    columns = [jnp.broadcast_to(live[8:, k : k + 1], (n - 8, n)) for k in range(8)]
    left = {(i, k): copies(heads[k][i : i + 1, :]) for k in range(8) for i in range(k, 8)}
    lower, scale = {}, []
    for j in range(8):
        scale.append(lax.rsqrt(left[j, j]))
        for i in range(j + 1, 8):
            lower[i, j] = left[i, j] * scale[j]
        for k in range(j + 1, 8):
            for i in range(k, 8):
                left[i, k] = left[i, k] - lower[i, j] * lower[k, j]
    done = []
    for j in range(8):
        value = copies(jnp.where(lanes < 8, jnp.where(lanes == j, 1.0, 0.0), top[j : j + 1, :]))
        for k in range(j):
            value = value - lower[j, k] * done[k]
        done.append(value * scale[j])
    solved = [None] * 8
    for k in reversed(range(8)):
        value = done[k]
        for j in range(k + 1, 8):
            value = value - lower[j, k] * solved[j]
        solved[k] = value * scale[k]
    rest = jnp.where(active[8:] & (lanes < 8), 0.0, c[8:])
    for k in range(8):
        rest = rest - columns[k] * solved[k][:1]
    top = jnp.concatenate([row[:1] for row in done], axis=0)
    return jnp.concatenate([pltpu.roll(rest, n - 8, 1), pltpu.roll(top, n - 8, 1)], axis=0)


def inverse_factor(c):
    n = c.shape[0]
    rows = lax.broadcasted_iota(jnp.int32, (n, n), 0)
    lanes = lax.broadcasted_iota(jnp.int32, (n, n), 1)
    return jnp.where(lanes <= rows, c, 0.0)


def times_transposed(a, b):
    a_high, a_low = halves(a)
    b_high, b_low = halves(b)
    return dot(
        jnp.concatenate([a_high, a_low, a_high], axis=1), jnp.concatenate([b_high, b_high, b_low], axis=1), ((1,), (1,))
    )


def exchange(
    g_hbm, e_hbm, q_hbm, m_v, right_out, p_hat_out,
    q_v, t_v, part_v, a_rx, by_rx, bz_rx, dz_rx, dy_rx, mean_v, p2_v,
    qp_v, rx_rx, ry_v, ry_rx, right_v, c_v,
    q_sem, load_sem, a_s, a_r, by_s, by_r, bz_s, bz_r, dz_s, dz_r, dy_s, dy_r, c_s, c_r,
    rx_s, rx_r, ry_s, ry_r, gy_s, gy_r, gx_s, gx_r,
):
    _, rows, width = m_v.shape
    rank = q_v.shape[1]
    chunk = rows // (NX * NC)
    cols = width // NX
    replicas = NX * NY
    nxc = NX * NC
    dp = lax.axis_index("dp")
    mp = lax.axis_index("mp")
    y, x, z, core = lax.div(dp, NX), lax.rem(dp, NX), lax.div(mp, NC), lax.rem(mp, NC)

    def device(y, x, z, core):
        return (y * NX + x, z * NC + core)

    def send(src, dst, s, r, to):
        pltpu.make_async_remote_copy(
            src_ref=src, dst_ref=dst, send_sem=s, recv_sem=r, device_id=to, device_id_type=MESH
        ).start()

    def wait(ref, sem):
        pltpu.make_async_copy(ref, ref, sem).wait()

    def along_y(i):
        k = far_first(i, NY)
        return k, device(lax.rem(y + k, NY), x, z, core)

    def along_z(i):
        k = far_first(i, NZ)
        return k, device(y, x, lax.rem(z + k, NZ), core)

    def across(i):
        x2 = lax.rem(x + far_first(lax.div(i, NC), NX), NX)
        c2 = lax.rem(core + NC - 1 - lax.rem(i, NC), NC)
        return x2 * NC + c2, device(y, x2, z, c2)

    def load(i):
        block = span(i * BLOCK, BLOCK, 16)
        return [
            pltpu.make_async_copy(src.at[block], m_v.at[k, block], load_sem.at[k, i])
            for k, src in enumerate((g_hbm, e_hbm))
        ]

    q_load = pltpu.make_async_copy(q_hbm, q_v, q_sem)
    q_load.start()
    loop(rows // BLOCK, lambda i: [copy.start() for copy in load(i)])

    barrier = pltpu.get_barrier_semaphore()

    def greet(to):
        pl.semaphore_signal(barrier, inc=1, device_id=to, device_id_type=MESH)

    loop(max(NY, NZ) - 1, lambda i: (greet(along_y(i)[1]), greet(along_z(i)[1])))
    loop(nxc - 1, lambda i: greet(across(i)[1]))

    q_load.wait()
    q2 = jnp.concatenate(halves(q_v[...]), axis=1)

    def left_rows(i):
        block = span(i * BLOCK, BLOCK, 16)
        for copy in load(i):
            copy.wait()
        both = dot(m_v[0, block, :], q2) + dot(m_v[1, block, :], q2)
        part_v[block, :] = both[:, :rank] + both[:, rank:]

    loop(rows // BLOCK, left_rows)

    pl.semaphore_wait(barrier, NY + NZ + nxc - 3)

    mine = x * NC + core

    def scatter(i):
        other, to = across(i)
        send(part_v.at[span(other * chunk, chunk)], a_rx.at[i], a_s, a_r.at[i], to)

    loop(nxc - 1, scatter)

    full = width // 128

    def turn(i):
        at = span(lax.rem(i, full) * 128, 128, 128)
        t_v[lax.div(i, full), at, :] = m_v[lax.div(i, full), :, at].T

    loop(2 * full, turn)
    if width % 128:

        def turn_rest(i):
            t_v[i, full * 128 :, :] = m_v[i, :, full * 128 :].T

        loop(2, turn_rest)

    def add_chunk(i, total):
        wait(a_rx.at[i], a_r.at[i])
        return total + a_rx[i]

    total = lax.fori_loop(0, nxc - 1, add_chunk, part_v[span(mine * chunk, chunk), :])

    def spread_y(ref, s, r, i):
        send(ref.at[y], ref.at[y], s, r, along_y(i)[1])

    def spread_z(ref, s, r, i):
        send(ref.at[z], ref.at[z], s, r, along_z(i)[1])

    def collect(ref, r):
        n = ref.shape[0]
        wait(ref.at[: n - 1], r)
        value = ref[0]
        for k in range(1, n):
            value = value + ref[k]
        return value

    by_rx[y] = total[:SPLIT]
    bz_rx[z] = total[SPLIT:]

    def spread(i):
        spread_y(by_rx, by_s, by_r, i)
        spread_z(bz_rx, bz_s, bz_r, i)

    loop(max(NY, NZ) - 1, spread)
    dz_rx[z] = collect(by_rx, by_r)
    loop(NZ - 1, functools.partial(spread_z, dz_rx, dz_s, dz_r))
    dy_rx[y] = collect(bz_rx, bz_r)
    loop(NY - 1, functools.partial(spread_y, dy_rx, dy_s, dy_r))
    mean_v[span(mine * chunk, SPLIT), :] = collect(dz_rx, dz_r) / replicas
    mean_v[span(mine * chunk + SPLIT, chunk - SPLIT), :] = collect(dy_rx, dy_r) / replicas

    own = mean_v.at[span(mine * chunk, chunk)]
    loop(nxc - 1, lambda i: send(own, own, c_s, c_r, across(i)[1]))

    wait(part_v.at[pl.ds(0, (nxc - 1) * chunk)], a_s)
    wait(by_rx.at[: NY - 1], by_s)
    wait(bz_rx.at[: NZ - 1], bz_s)
    wait(dz_rx.at[: NZ - 1], dz_s)
    wait(dy_rx.at[: NY - 1], dy_s)
    wait(mean_v.at[pl.ds(0, (nxc - 1) * chunk)], c_r)
    wait(mean_v.at[pl.ds(0, (nxc - 1) * chunk)], c_s)
    p2_v[...] = jnp.concatenate(halves(mean_v[...]), axis=1)

    def right_rows(i):
        block = span(i * TALL, TALL, 16)
        both = dot(t_v[0, block, :], p2_v[...]) + dot(t_v[1, block, :], p2_v[...])
        qp_v[block, :] = both[:, :rank] + both[:, rank:]

    loop(width // TALL, right_rows)

    def for_piece(y, body):
        pl.when(y < MORE)(lambda: body(y * LONG, LONG))
        pl.when(y >= MORE)(lambda: body(y * PIECE + MORE * (LONG - PIECE), PIECE))

    def whole(x, start, size):
        return span(x * cols + start, size)

    def along_x(i):
        k = far_first(i, NX)
        return k - 1, lax.rem(x + k, NX), device(y, lax.rem(x + k, NX), z, core)

    def scatter_x(i):
        ky = far_first(i, NY)

        def body(start, size):
            def step(j):
                kx, x2, to = along_x(j)
                send(qp_v.at[whole(x2, start, size)], rx_rx.at[kx, span(start, size)], rx_s, rx_r.at[kx, ky], to)

            loop(NX - 1, step)

        for_piece(lax.rem(y + ky, NY), body)

    loop(NY, scatter_x)
    mean = mean_v[...]
    c_v[...] = dot(mean, mean, ((0,), (0,)), lax.Precision.HIGHEST)

    def scatter_y(i):
        ky = far_first(i, NY)

        def body(start, size):
            part = span(start, size)
            value = qp_v[whole(x, start, size), :]
            for kx in range(NX - 1):
                wait(rx_rx.at[kx, part], rx_r.at[kx, ky])
                value = value + rx_rx[kx, part, :]
            ry_v[part, :] = value

            @pl.when(ky > 0)
            def _():
                dst = ry_rx.at[ky - 1, pl.ds(0, size)]
                send(ry_v.at[part], dst, ry_s, ry_r.at[ky - 1], along_y(i)[1])

        for_piece(lax.rem(y + ky, NY), body)

    steps = rank // 8

    def stage(i):
        first = jnp.where(i == 0, 0, FIRST + i - 1)
        last = jnp.where(i == NY, steps, FIRST + i)
        c_v[...] = lax.fori_loop(first, last, panel, c_v[...])

        @pl.when(i < NY)
        def _():
            scatter_y(i)

    loop(NY + 1, stage)
    inverse = inverse_factor(c_v[...])

    def to_x(ref):
        loop(NX - 1, lambda j: send(ref, ref, gx_s, gx_r, along_x(j)[2]))

    def gather_own(start, size):
        def add(i, value):
            wait(ry_rx.at[i, pl.ds(0, size)], ry_r.at[i])
            return value + ry_rx[i, :size]

        total = lax.fori_loop(0, NY - 1, add, ry_v[span(start, size), :])
        right_v[whole(x, start, size), :] = times_transposed(total, inverse) / replicas
        out = right_v.at[whole(x, start, size)]
        to_x(out)
        loop(NY - 1, lambda i: send(out, out, gy_s, gy_r.at[along_y(i)[0] - 1], along_y(i)[1]))

    for_piece(y, gather_own)
    p_hat_out[...] = times_transposed(mean_v[...], inverse)
    sent = qp_v.at[pl.ds(0, (NX - 1) * cols)]
    wait(sent, rx_s)

    def pass_on(i):
        ky = far_first(NY - 2 - i, NY)

        def body(start, size):
            got = right_v.at[whole(x, start, size)]
            wait(got, gy_r.at[ky - 1])
            to_x(got)

        for_piece(lax.rem(y + NY - ky, NY), body)

    loop(NY - 1, pass_on)

    def sent_along_y(start, size):
        wait(ry_v.at[pl.ds(0, cols - size)], ry_s)
        wait(qp_v.at[pl.ds(0, (NY - 1) * size)], gy_s)

    for_piece(y, sent_along_y)
    wait(sent, gx_r)
    wait(sent, gx_s)
    right_out[...] = right_v[...]


def finish(
    m_v, q_v, p_hat_v, approx_hbm, q_hbm, error_hbm,
    q3_v, approx_v, error_v, q_sem, sems,
):
    _, rows, width = m_v.shape

    q_copy = pltpu.make_async_copy(q_v, q_hbm, q_sem)
    q_copy.start()

    def right_rows(i):
        block = span(i * TALL, TALL, 16)
        high, low = halves(q_v[block, :])
        q3_v[block, :] = jnp.concatenate([high, high, low], axis=1)

    loop(width // TALL, right_rows)

    def stores(i):
        block = span(i * BLOCK, BLOCK, 16)
        return [
            pltpu.make_async_copy(src.at[block], dst.at[block], sems.at[k, i])
            for k, (src, dst) in enumerate(((approx_v, approx_hbm), (error_v, error_hbm)))
        ]

    def left_rows(i):
        block = span(i * BLOCK, BLOCK, 16)
        high, low = halves(p_hat_v[block, :])
        full = dot(jnp.concatenate([high, low, high], axis=1), q3_v[...], ((1,), (1,)))
        approx_v[block, :] = full.astype(BF16)
        error_v[block, :] = (m_v[0, block, :].astype(F32) + m_v[1, block, :].astype(F32) - full).astype(BF16)
        for copy in stores(i):
            copy.start()

    loop(rows // BLOCK, left_rows)
    loop(rows // BLOCK, lambda i: [copy.wait() for copy in stores(i)])
    q_copy.wait()


def local(grads, errors, q_start):
    grads, errors = grads[0], errors[0]
    rows, width = grads.shape
    rank = q_start.shape[1]
    chunk = rows // (NX * NC)
    cols = width // NX
    nxc = NX * NC - 1
    anywhere = pl.BlockSpec(memory_space=pl.ANY)
    vmem = pl.BlockSpec(memory_space=pltpu.VMEM)
    dma = pltpu.SemaphoreType.DMA
    merged, right, p_hat = pl.pallas_call(
        exchange,
        out_shape=(
            pltpu.VMEM((2, rows, width), BF16),
            pltpu.VMEM((width, rank), F32),
            pltpu.VMEM((rows, rank), F32),
        ),
        in_specs=[anywhere] * 3,
        out_specs=(vmem,) * 3,
        scratch_shapes=[
            pltpu.VMEM((width, rank), F32),
            pltpu.VMEM((2, width, rows), BF16),
            pltpu.VMEM((rows, rank), F32),
            pltpu.VMEM((nxc, chunk, rank), F32),
            pltpu.VMEM((NY, SPLIT, rank), F32),
            pltpu.VMEM((NZ, chunk - SPLIT, rank), F32),
            pltpu.VMEM((NZ, SPLIT, rank), F32),
            pltpu.VMEM((NY, chunk - SPLIT, rank), F32),
            pltpu.VMEM((rows, rank), F32),
            pltpu.VMEM((rows, 2 * rank), BF16),
            pltpu.VMEM((width, rank), F32),
            pltpu.VMEM((NX - 1, cols, rank), F32),
            pltpu.VMEM((cols, rank), F32),
            pltpu.VMEM((NY - 1, LONG, rank), F32),
            pltpu.VMEM((width, rank), F32),
            pltpu.VMEM((rank, rank), F32),
            dma, dma((2, rows // BLOCK)),
            dma, dma((nxc,)),
            dma, dma, dma, dma, dma, dma, dma, dma,
            dma, dma,
            dma, dma((NX - 1, NY)),
            dma, dma((NY - 1,)),
            dma, dma((NY - 1,)),
            dma, dma,
        ],
        compiler_params=pltpu.CompilerParams(collective_id=0, has_side_effects=True, vmem_limit_bytes=LIMIT),
        name="exchange",
    )(grads, errors, q_start)

    approx, q_next, error_next = pl.pallas_call(
        finish,
        out_shape=(
            jax.ShapeDtypeStruct((rows, width), BF16),
            jax.ShapeDtypeStruct((width, rank), F32),
            jax.ShapeDtypeStruct((rows, width), BF16),
        ),
        in_specs=[vmem] * 3,
        out_specs=(anywhere,) * 3,
        scratch_shapes=[
            pltpu.VMEM((width, 3 * rank), BF16),
            pltpu.VMEM((rows, width), BF16),
            pltpu.VMEM((rows, width), BF16),
            dma,
            dma((2, rows // BLOCK)),
        ],
        compiler_params=pltpu.CompilerParams(vmem_limit_bytes=LIMIT - 2**20),
        name="finish",
    )(merged, right, p_hat)
    return approx, q_next, error_next[None]


def solution(mesh):
    return jax.shard_map(
        local,
        mesh=mesh,
        in_specs=(P("dp", None, "mp"), P("dp", None, "mp"), P("mp", None)),
        out_specs=(P(None, "mp"), P("mp", None), P("dp", None, "mp")),
        check_vma=False,
    )
```

```python
import functools

import jax
import jax.numpy as jnp
from jax import lax
from jax.experimental import pallas as pl
from jax.experimental.pallas import tpu as pltpu
from jax.sharding import PartitionSpec as P

MESH = pl.DeviceIdType.MESH
F32 = jnp.float32
BF16 = jnp.bfloat16

NX, NY, NZ, NC = 4, 8, 8, 2
PIECE, LONG, MORE = 32, 40, 3
SPLIT = 32
BLOCK = 112
TALL = 224
FIRST = 5
WIDE = 256
LIMIT = 51 * 2**20


def loop(n, body):
    def step(i, carry):
        body(i)
        return carry

    lax.fori_loop(0, n, step, 0)


def far_first(i, n):
    return n // 2 + lax.div(i + 1, 2) * (1 - 2 * lax.rem(i, 2))


def dot(a, b, dims=((1,), (0,)), precision=None):
    return lax.dot_general(a, b, (dims, ((), ())), precision=precision, preferred_element_type=F32)


def halves(a):
    high = a.astype(BF16)
    return high, (a - high.astype(F32)).astype(BF16)


def span(start, size, unit=8):
    return pl.ds(pl.multiple_of(start, unit), size)


def panel(index, c):
    n = c.shape[0]
    lanes = lax.broadcasted_iota(jnp.int32, (1, n), 1)
    rows = lax.broadcasted_iota(jnp.int32, (n, 1), 0)
    active = rows < n - 8 * index
    live = jnp.where(active, c, 0.0)
    top = c[:8, :]

    def copies(row):
        return jnp.broadcast_to(row, (8, n))

    heads = [jnp.broadcast_to(top[:, k : k + 1], (8, n)) for k in range(8)]
    columns = [jnp.broadcast_to(live[8:, k : k + 1], (n - 8, n)) for k in range(8)]
    left = {(i, k): copies(heads[k][i : i + 1, :]) for k in range(8) for i in range(k, 8)}
    lower, scale = {}, []
    for j in range(8):
        scale.append(lax.rsqrt(left[j, j]))
        for i in range(j + 1, 8):
            lower[i, j] = left[i, j] * scale[j]
        for k in range(j + 1, 8):
            for i in range(k, 8):
                left[i, k] = left[i, k] - lower[i, j] * lower[k, j]
    done = []
    for j in range(8):
        value = copies(jnp.where(lanes < 8, jnp.where(lanes == j, 1.0, 0.0), top[j : j + 1, :]))
        for k in range(j):
            value = value - lower[j, k] * done[k]
        done.append(value * scale[j])
    solved = [None] * 8
    for k in reversed(range(8)):
        value = done[k]
        for j in range(k + 1, 8):
            value = value - lower[j, k] * solved[j]
        solved[k] = value * scale[k]
    rest = jnp.where(active[8:] & (lanes < 8), 0.0, c[8:])
    for k in range(8):
        rest = rest - columns[k] * solved[k][:1]
    top = jnp.concatenate([row[:1] for row in done], axis=0)
    return jnp.concatenate([pltpu.roll(rest, n - 8, 1), pltpu.roll(top, n - 8, 1)], axis=0)


def inverse_factor(c):
    n = c.shape[0]
    rows = lax.broadcasted_iota(jnp.int32, (n, n), 0)
    lanes = lax.broadcasted_iota(jnp.int32, (n, n), 1)
    return jnp.where(lanes <= rows, c, 0.0)


def times_transposed(a, b):
    a_high, a_low = halves(a)
    b_high, b_low = halves(b)
    return dot(
        jnp.concatenate([a_high, a_low, a_high], axis=1), jnp.concatenate([b_high, b_high, b_low], axis=1), ((1,), (1,))
    )


def exchange(
    g_hbm, e_hbm, q_hbm, m_v, right_out, p_hat_out,
    q_v, t_v, part_v, a_rx, by_rx, bz_rx, dz_rx, dy_rx, mean_v, p2_v,
    qp_v, rx_rx, ry_v, ry_rx, right_v, c_v,
    q_sem, load_sem, a_s, a_r, by_s, by_r, bz_s, bz_r, dz_s, dz_r, dy_s, dy_r, c_s, c_r,
    rx_s, rx_r, ry_s, ry_r, gy_s, gy_r, gx_s, gx_r,
):
    _, rows, width = m_v.shape
    rank = q_v.shape[1]
    chunk = rows // (NX * NC)
    cols = width // NX
    replicas = NX * NY
    nxc = NX * NC
    dp = lax.axis_index("dp")
    mp = lax.axis_index("mp")
    y, x, z, core = lax.div(dp, NX), lax.rem(dp, NX), lax.div(mp, NC), lax.rem(mp, NC)

    def device(y, x, z, core):
        return (y * NX + x, z * NC + core)

    def send(src, dst, s, r, to):
        pltpu.make_async_remote_copy(
            src_ref=src, dst_ref=dst, send_sem=s, recv_sem=r, device_id=to, device_id_type=MESH
        ).start()

    def wait(ref, sem):
        pltpu.make_async_copy(ref, ref, sem).wait()

    def along_y(i):
        k = far_first(i, NY)
        return k, device(lax.rem(y + k, NY), x, z, core)

    def along_z(i):
        k = far_first(i, NZ)
        return k, device(y, x, lax.rem(z + k, NZ), core)

    def across(i):
        x2 = lax.rem(x + far_first(lax.div(i, NC), NX), NX)
        c2 = lax.rem(core + NC - 1 - lax.rem(i, NC), NC)
        return x2 * NC + c2, device(y, x2, z, c2)

    def load(i):
        block = span(i * BLOCK, BLOCK, 16)
        return [
            pltpu.make_async_copy(src.at[block], m_v.at[k, block], load_sem.at[k, i])
            for k, src in enumerate((g_hbm, e_hbm))
        ]

    q_load = pltpu.make_async_copy(q_hbm, q_v, q_sem)
    q_load.start()
    loop(rows // BLOCK, lambda i: [copy.start() for copy in load(i)])

    barrier = pltpu.get_barrier_semaphore()

    def greet(to):
        pl.semaphore_signal(barrier, inc=1, device_id=to, device_id_type=MESH)

    loop(max(NY, NZ) - 1, lambda i: (greet(along_y(i)[1]), greet(along_z(i)[1])))
    loop(nxc - 1, lambda i: greet(across(i)[1]))

    q_load.wait()
    q2 = jnp.concatenate(halves(q_v[...]), axis=1)

    def left_rows(i):
        block = span(i * BLOCK, BLOCK, 16)
        for copy in load(i):
            copy.wait()
        both = dot(m_v[0, block, :], q2) + dot(m_v[1, block, :], q2)
        part_v[block, :] = both[:, :rank] + both[:, rank:]

    loop(rows // BLOCK, left_rows)

    pl.semaphore_wait(barrier, NY + NZ + nxc - 3)

    mine = x * NC + core

    def scatter(i):
        other, to = across(i)
        send(part_v.at[span(other * chunk, chunk)], a_rx.at[i], a_s, a_r.at[i], to)

    loop(nxc - 1, scatter)

    full = width // 128

    def turn(i):
        at = span(lax.rem(i, full) * 128, 128, 128)
        t_v[lax.div(i, full), at, :] = m_v[lax.div(i, full), :, at].T

    loop(2 * full, turn)
    if width % 128:

        def turn_rest(i):
            t_v[i, full * 128 :, :] = m_v[i, :, full * 128 :].T

        loop(2, turn_rest)

    def add_chunk(i, total):
        wait(a_rx.at[i], a_r.at[i])
        return total + a_rx[i]

    total = lax.fori_loop(0, nxc - 1, add_chunk, part_v[span(mine * chunk, chunk), :])

    def spread_y(ref, s, r, i):
        send(ref.at[y], ref.at[y], s, r, along_y(i)[1])

    def spread_z(ref, s, r, i):
        send(ref.at[z], ref.at[z], s, r, along_z(i)[1])

    def collect(ref, r):
        n = ref.shape[0]
        wait(ref.at[: n - 1], r)
        value = ref[0]
        for k in range(1, n):
            value = value + ref[k]
        return value

    by_rx[y] = total[:SPLIT]
    bz_rx[z] = total[SPLIT:]

    def spread(i):
        spread_y(by_rx, by_s, by_r, i)
        spread_z(bz_rx, bz_s, bz_r, i)

    loop(max(NY, NZ) - 1, spread)
    dz_rx[z] = collect(by_rx, by_r)
    loop(NZ - 1, functools.partial(spread_z, dz_rx, dz_s, dz_r))
    dy_rx[y] = collect(bz_rx, bz_r)
    loop(NY - 1, functools.partial(spread_y, dy_rx, dy_s, dy_r))
    mean_v[span(mine * chunk, SPLIT), :] = collect(dz_rx, dz_r) / replicas
    mean_v[span(mine * chunk + SPLIT, chunk - SPLIT), :] = collect(dy_rx, dy_r) / replicas

    own = mean_v.at[span(mine * chunk, chunk)]
    loop(nxc - 1, lambda i: send(own, own, c_s, c_r, across(i)[1]))

    wait(part_v.at[pl.ds(0, (nxc - 1) * chunk)], a_s)
    wait(by_rx.at[: NY - 1], by_s)
    wait(bz_rx.at[: NZ - 1], bz_s)
    wait(dz_rx.at[: NZ - 1], dz_s)
    wait(dy_rx.at[: NY - 1], dy_s)
    wait(mean_v.at[pl.ds(0, (nxc - 1) * chunk)], c_r)
    wait(mean_v.at[pl.ds(0, (nxc - 1) * chunk)], c_s)
    p2_v[...] = jnp.concatenate(halves(mean_v[...]), axis=1)

    def right_rows(i):
        block = span(i * TALL, TALL, 16)
        both = dot(t_v[:, block, :].reshape(2 * TALL, rows), p2_v[...])
        both = both[:TALL] + both[TALL:]
        qp_v[block, :] = both[:, :rank] + both[:, rank:]

    loop(width // TALL, right_rows)

    def for_piece(y, body):
        pl.when(y < MORE)(lambda: body(y * LONG, LONG))
        pl.when(y >= MORE)(lambda: body(y * PIECE + MORE * (LONG - PIECE), PIECE))

    def whole(x, start, size):
        return span(x * cols + start, size)

    def along_x(i):
        k = far_first(i, NX)
        return k - 1, lax.rem(x + k, NX), device(y, lax.rem(x + k, NX), z, core)

    def scatter_x(i):
        ky = far_first(i, NY)

        def body(start, size):
            def step(j):
                kx, x2, to = along_x(j)
                send(qp_v.at[whole(x2, start, size)], rx_rx.at[kx, span(start, size)], rx_s, rx_r.at[kx, ky], to)

            loop(NX - 1, step)

        for_piece(lax.rem(y + ky, NY), body)

    loop(NY, scatter_x)
    mean = mean_v[...]
    c_v[...] = dot(mean, mean, ((0,), (0,)), lax.Precision.HIGHEST)

    def scatter_y(i):
        ky = far_first(i, NY)

        def body(start, size):
            part = span(start, size)
            value = qp_v[whole(x, start, size), :]
            for kx in range(NX - 1):
                wait(rx_rx.at[kx, part], rx_r.at[kx, ky])
                value = value + rx_rx[kx, part, :]
            ry_v[part, :] = value

            @pl.when(ky > 0)
            def _():
                dst = ry_rx.at[ky - 1, pl.ds(0, size)]
                send(ry_v.at[part], dst, ry_s, ry_r.at[ky - 1], along_y(i)[1])

        for_piece(lax.rem(y + ky, NY), body)

    steps = rank // 8

    def stage(i):
        first = jnp.where(i == 0, 0, FIRST + i - 1)
        last = jnp.where(i == NY, steps, FIRST + i)
        c_v[...] = lax.fori_loop(first, last, panel, c_v[...])

        @pl.when(i < NY)
        def _():
            scatter_y(i)

    loop(NY + 1, stage)
    inverse = inverse_factor(c_v[...])

    def to_x(ref):
        loop(NX - 1, lambda j: send(ref, ref, gx_s, gx_r, along_x(j)[2]))

    def gather_own(start, size):
        def add(i, value):
            wait(ry_rx.at[i, pl.ds(0, size)], ry_r.at[i])
            return value + ry_rx[i, :size]

        total = lax.fori_loop(0, NY - 1, add, ry_v[span(start, size), :])
        right_v[whole(x, start, size), :] = times_transposed(total, inverse) / replicas
        out = right_v.at[whole(x, start, size)]
        to_x(out)
        loop(NY - 1, lambda i: send(out, out, gy_s, gy_r.at[along_y(i)[0] - 1], along_y(i)[1]))

    for_piece(y, gather_own)
    p_hat_out[...] = times_transposed(mean_v[...], inverse)
    sent = qp_v.at[pl.ds(0, (NX - 1) * cols)]
    wait(sent, rx_s)

    def pass_on(i):
        ky = far_first(NY - 2 - i, NY)

        def body(start, size):
            got = right_v.at[whole(x, start, size)]
            wait(got, gy_r.at[ky - 1])
            to_x(got)

        for_piece(lax.rem(y + NY - ky, NY), body)

    loop(NY - 1, pass_on)

    def sent_along_y(start, size):
        wait(ry_v.at[pl.ds(0, cols - size)], ry_s)
        wait(qp_v.at[pl.ds(0, (NY - 1) * size)], gy_s)

    for_piece(y, sent_along_y)
    wait(sent, gx_r)
    wait(sent, gx_s)
    right_out[...] = right_v[...]


def finish(
    m_v, q_v, p_hat_v, approx_hbm, q_hbm, error_hbm,
    p3_v, approx_v, error_v, q_sem, sems,
):
    _, rows, width = m_v.shape
    q_copy = pltpu.make_async_copy(q_v, q_hbm, q_sem)
    q_copy.start()
    high, low = halves(p_hat_v[...])
    p3_v[...] = jnp.concatenate([high, low, high], axis=1)

    def stores(i, columns):
        return [
            pltpu.make_async_copy(src.at[:, columns], dst.at[:, columns], sems.at[k, i])
            for k, (src, dst) in enumerate(((approx_v, approx_hbm), (error_v, error_hbm)))
        ]

    def tile(i, columns):
        high, low = halves(q_v[columns, :])
        full = dot(p3_v[...], jnp.concatenate([high, high, low], axis=1), ((1,), (1,)))
        approx_v[:, columns] = full.astype(BF16)
        error_v[:, columns] = (m_v[0, :, columns].astype(F32) + m_v[1, :, columns].astype(F32) - full).astype(BF16)
        for copy in stores(i, columns):
            copy.start()

    tiles = width // WIDE
    rest = pl.ds(tiles * WIDE, width - tiles * WIDE)
    tile(tiles, rest)
    loop(tiles, lambda i: tile(i, span(i * WIDE, WIDE, 128)))
    loop(tiles, lambda i: [copy.wait() for copy in stores(i, span(i * WIDE, WIDE, 128))])
    for copy in stores(tiles, rest):
        copy.wait()
    q_copy.wait()


def local(grads, errors, q_start):
    grads, errors = grads[0], errors[0]
    rows, width = grads.shape
    rank = q_start.shape[1]
    chunk = rows // (NX * NC)
    cols = width // NX
    nxc = NX * NC - 1
    anywhere = pl.BlockSpec(memory_space=pl.ANY)
    vmem = pl.BlockSpec(memory_space=pltpu.VMEM)
    dma = pltpu.SemaphoreType.DMA
    merged, right, p_hat = pl.pallas_call(
        exchange,
        out_shape=(
            pltpu.VMEM((2, rows, width), BF16),
            pltpu.VMEM((width, rank), F32),
            pltpu.VMEM((rows, rank), F32),
        ),
        in_specs=[anywhere] * 3,
        out_specs=(vmem,) * 3,
        scratch_shapes=[
            pltpu.VMEM((width, rank), F32),
            pltpu.VMEM((2, width, rows), BF16),
            pltpu.VMEM((rows, rank), F32),
            pltpu.VMEM((nxc, chunk, rank), F32),
            pltpu.VMEM((NY, SPLIT, rank), F32),
            pltpu.VMEM((NZ, chunk - SPLIT, rank), F32),
            pltpu.VMEM((NZ, SPLIT, rank), F32),
            pltpu.VMEM((NY, chunk - SPLIT, rank), F32),
            pltpu.VMEM((rows, rank), F32),
            pltpu.VMEM((rows, 2 * rank), BF16),
            pltpu.VMEM((width, rank), F32),
            pltpu.VMEM((NX - 1, cols, rank), F32),
            pltpu.VMEM((cols, rank), F32),
            pltpu.VMEM((NY - 1, LONG, rank), F32),
            pltpu.VMEM((width, rank), F32),
            pltpu.VMEM((rank, rank), F32),
            dma, dma((2, rows // BLOCK)),
            dma, dma((nxc,)),
            dma, dma, dma, dma, dma, dma, dma, dma,
            dma, dma,
            dma, dma((NX - 1, NY)),
            dma, dma((NY - 1,)),
            dma, dma((NY - 1,)),
            dma, dma,
        ],
        compiler_params=pltpu.CompilerParams(collective_id=0, has_side_effects=True, vmem_limit_bytes=LIMIT),
        name="exchange",
    )(grads, errors, q_start)

    approx, q_next, error_next = pl.pallas_call(
        finish,
        out_shape=(
            jax.ShapeDtypeStruct((rows, width), BF16),
            jax.ShapeDtypeStruct((width, rank), F32),
            jax.ShapeDtypeStruct((rows, width), BF16),
        ),
        in_specs=[vmem] * 3,
        out_specs=(anywhere,) * 3,
        scratch_shapes=[
            pltpu.VMEM((rows, 3 * rank), BF16),
            pltpu.VMEM((rows, width), BF16),
            pltpu.VMEM((rows, width), BF16),
            dma,
            dma((2, width // WIDE + 1)),
        ],
        compiler_params=pltpu.CompilerParams(vmem_limit_bytes=LIMIT - 2**20),
        name="finish",
    )(merged, right, p_hat)
    return approx, q_next, error_next[None]


def solution(mesh):
    return jax.shard_map(
        local,
        mesh=mesh,
        in_specs=(P("dp", None, "mp"), P("dp", None, "mp"), P("mp", None)),
        out_specs=(P(None, "mp"), P("mp", None), P("dp", None, "mp")),
        check_vma=False,
    )
```

```python
import functools

import jax
import jax.numpy as jnp
from jax import lax
from jax.experimental import pallas as pl
from jax.experimental.pallas import tpu as pltpu
from jax.sharding import PartitionSpec as P

MESH = pl.DeviceIdType.MESH
F32 = jnp.float32
BF16 = jnp.bfloat16

NX, NY, NZ, NC = 4, 8, 8, 2
PIECE, LONG, MORE = 32, 40, 3
SPLIT = 32
BLOCK = 112
TALL = 224
FIRST = 5
WIDE = 256
LIMIT = 51 * 2**20


def loop(n, body):
    def step(i, carry):
        body(i)
        return carry

    lax.fori_loop(0, n, step, 0)


def far_first(i, n):
    return n // 2 + lax.div(i + 1, 2) * (1 - 2 * lax.rem(i, 2))


def dot(a, b, dims=((1,), (0,)), precision=None):
    return lax.dot_general(a, b, (dims, ((), ())), precision=precision, preferred_element_type=F32)


def halves(a):
    high = a.astype(BF16)
    return high, (a - high.astype(F32)).astype(BF16)


def span(start, size, unit=8):
    return pl.ds(pl.multiple_of(start, unit), size)


def panel(index, c):
    n = c.shape[0]
    lanes = lax.broadcasted_iota(jnp.int32, (1, n), 1)
    rows = lax.broadcasted_iota(jnp.int32, (n, 1), 0)
    active = rows < n - 8 * index
    live = jnp.where(active, c, 0.0)
    top = c[:8, :]

    def copies(row):
        return jnp.broadcast_to(row, (8, n))

    heads = [jnp.broadcast_to(top[:, k : k + 1], (8, n)) for k in range(8)]
    columns = [jnp.broadcast_to(live[8:, k : k + 1], (n - 8, n)) for k in range(8)]
    left = {(i, k): copies(heads[k][i : i + 1, :]) for k in range(8) for i in range(k, 8)}
    lower, scale = {}, []
    for j in range(8):
        scale.append(lax.rsqrt(left[j, j]))
        for i in range(j + 1, 8):
            lower[i, j] = left[i, j] * scale[j]
        for k in range(j + 1, 8):
            for i in range(k, 8):
                left[i, k] = left[i, k] - lower[i, j] * lower[k, j]
    done = []
    for j in range(8):
        value = copies(jnp.where(lanes < 8, jnp.where(lanes == j, 1.0, 0.0), top[j : j + 1, :]))
        for k in range(j):
            value = value - lower[j, k] * done[k]
        done.append(value * scale[j])
    solved = [None] * 8
    for k in reversed(range(8)):
        value = done[k]
        for j in range(k + 1, 8):
            value = value - lower[j, k] * solved[j]
        solved[k] = value * scale[k]
    rest = jnp.where(active[8:] & (lanes < 8), 0.0, c[8:])
    for k in range(8):
        rest = rest - columns[k] * solved[k][:1]
    top = jnp.concatenate([row[:1] for row in done], axis=0)
    return jnp.concatenate([pltpu.roll(rest, n - 8, 1), pltpu.roll(top, n - 8, 1)], axis=0)


def inverse_factor(c):
    n = c.shape[0]
    rows = lax.broadcasted_iota(jnp.int32, (n, n), 0)
    lanes = lax.broadcasted_iota(jnp.int32, (n, n), 1)
    return jnp.where(lanes <= rows, c, 0.0)


def times_transposed(a, b):
    a_high, a_low = halves(a)
    b_high, b_low = halves(b)
    return dot(
        jnp.concatenate([a_high, a_low, a_high], axis=1), jnp.concatenate([b_high, b_high, b_low], axis=1), ((1,), (1,))
    )


def exchange(
    g_hbm, e_hbm, q_hbm, m_v, right_out, p_hat_out,
    q_v, t_v, part_v, a_rx, by_rx, bz_rx, dz_rx, dy_rx, mean_v, p2_v,
    qp_v, rx_rx, ry_v, ry_rx, right_v, c_v,
    q_sem, load_sem, a_s, a_r, by_s, by_r, bz_s, bz_r, dz_s, dz_r, dy_s, dy_r, c_s, c_r,
    rx_s, rx_r, ry_s, ry_r, gy_s, gy_r, gx_s, gx_r,
):
    _, rows, width = m_v.shape
    rank = q_v.shape[1]
    chunk = rows // (NX * NC)
    cols = width // NX
    replicas = NX * NY
    nxc = NX * NC
    dp = lax.axis_index("dp")
    mp = lax.axis_index("mp")
    y, x, z, core = lax.div(dp, NX), lax.rem(dp, NX), lax.div(mp, NC), lax.rem(mp, NC)

    def device(y, x, z, core):
        return (y * NX + x, z * NC + core)

    def send(src, dst, s, r, to):
        pltpu.make_async_remote_copy(
            src_ref=src, dst_ref=dst, send_sem=s, recv_sem=r, device_id=to, device_id_type=MESH
        ).start()

    def wait(ref, sem):
        pltpu.make_async_copy(ref, ref, sem).wait()

    def along_y(i):
        k = far_first(i, NY)
        return k, device(lax.rem(y + k, NY), x, z, core)

    def along_z(i):
        k = far_first(i, NZ)
        return k, device(y, x, lax.rem(z + k, NZ), core)

    def across(i):
        x2 = lax.rem(x + far_first(lax.div(i, NC), NX), NX)
        c2 = lax.rem(core + NC - 1 - lax.rem(i, NC), NC)
        return x2 * NC + c2, device(y, x2, z, c2)

    def load(i):
        block = span(i * BLOCK, BLOCK, 16)
        return [
            pltpu.make_async_copy(src.at[block], m_v.at[k, block], load_sem.at[k, i])
            for k, src in enumerate((g_hbm, e_hbm))
        ]

    q_load = pltpu.make_async_copy(q_hbm, q_v, q_sem)
    q_load.start()
    loop(rows // BLOCK, lambda i: [copy.start() for copy in load(i)])

    barrier = pltpu.get_barrier_semaphore()

    def greet(to):
        pl.semaphore_signal(barrier, inc=1, device_id=to, device_id_type=MESH)

    loop(max(NY, NZ) - 1, lambda i: (greet(along_y(i)[1]), greet(along_z(i)[1])))
    loop(nxc - 1, lambda i: greet(across(i)[1]))

    q_load.wait()
    q2 = jnp.concatenate(halves(q_v[...]), axis=1)

    def left_rows(i):
        block = span(i * BLOCK, BLOCK, 16)
        for copy in load(i):
            copy.wait()
        both = dot(m_v[0, block, :], q2) + dot(m_v[1, block, :], q2)
        part_v[block, :] = both[:, :rank] + both[:, rank:]

    loop(rows // BLOCK, left_rows)

    pl.semaphore_wait(barrier, NY + NZ + nxc - 3)

    mine = x * NC + core

    def scatter(i):
        other, to = across(i)
        send(part_v.at[span(other * chunk, chunk)], a_rx.at[i], a_s, a_r.at[i], to)

    loop(nxc - 1, scatter)

    full = width // 128

    def turn(i):
        at = span(lax.rem(i, full) * 128, 128, 128)
        t_v[lax.div(i, full), at, :] = m_v[lax.div(i, full), :, at].T

    loop(2 * full, turn)
    if width % 128:

        def turn_rest(i):
            t_v[i, full * 128 :, :] = m_v[i, :, full * 128 :].T

        loop(2, turn_rest)

    def add_chunk(i, total):
        wait(a_rx.at[i], a_r.at[i])
        return total + a_rx[i]

    total = lax.fori_loop(0, nxc - 1, add_chunk, part_v[span(mine * chunk, chunk), :])

    def spread_y(ref, s, r, i):
        send(ref.at[y], ref.at[y], s, r, along_y(i)[1])

    def spread_z(ref, s, r, i):
        send(ref.at[z], ref.at[z], s, r, along_z(i)[1])

    def collect(ref, r):
        n = ref.shape[0]
        wait(ref.at[: n - 1], r)
        value = ref[0]
        for k in range(1, n):
            value = value + ref[k]
        return value

    by_rx[y] = total[:SPLIT]
    bz_rx[z] = total[SPLIT:]

    def spread(i):
        spread_y(by_rx, by_s, by_r, i)
        spread_z(bz_rx, bz_s, bz_r, i)

    loop(max(NY, NZ) - 1, spread)
    dz_rx[z] = collect(by_rx, by_r)
    loop(NZ - 1, functools.partial(spread_z, dz_rx, dz_s, dz_r))
    dy_rx[y] = collect(bz_rx, bz_r)
    loop(NY - 1, functools.partial(spread_y, dy_rx, dy_s, dy_r))
    def gather(start, size, value):
        mean_v[span(start, size), :] = value / replicas
        own = mean_v.at[span(start, size)]
        loop(nxc - 1, lambda i: send(own, own, c_s, c_r, across(i)[1]))

    gather(mine * chunk, SPLIT, collect(dz_rx, dz_r))
    gather(mine * chunk + SPLIT, chunk - SPLIT, collect(dy_rx, dy_r))

    wait(part_v.at[pl.ds(0, (nxc - 1) * chunk)], a_s)
    wait(by_rx.at[: NY - 1], by_s)
    wait(bz_rx.at[: NZ - 1], bz_s)
    wait(dz_rx.at[: NZ - 1], dz_s)
    wait(dy_rx.at[: NY - 1], dy_s)
    wait(mean_v.at[pl.ds(0, (nxc - 1) * chunk)], c_r)
    wait(mean_v.at[pl.ds(0, (nxc - 1) * chunk)], c_s)
    p2_v[...] = jnp.concatenate(halves(mean_v[...]), axis=1)

    def right_rows(i):
        block = span(i * TALL, TALL, 16)
        both = dot(t_v[:, block, :].reshape(2 * TALL, rows), p2_v[...])
        both = both[:TALL] + both[TALL:]
        qp_v[block, :] = both[:, :rank] + both[:, rank:]

    loop(width // TALL, right_rows)

    def for_piece(y, body):
        pl.when(y < MORE)(lambda: body(y * LONG, LONG))
        pl.when(y >= MORE)(lambda: body(y * PIECE + MORE * (LONG - PIECE), PIECE))

    def whole(x, start, size):
        return span(x * cols + start, size)

    def along_x(i):
        k = far_first(i, NX)
        return k - 1, lax.rem(x + k, NX), device(y, lax.rem(x + k, NX), z, core)

    def scatter_x(i):
        ky = far_first(i, NY)

        def body(start, size):
            def step(j):
                kx, x2, to = along_x(j)
                send(qp_v.at[whole(x2, start, size)], rx_rx.at[kx, span(start, size)], rx_s, rx_r.at[kx, ky], to)

            loop(NX - 1, step)

        for_piece(lax.rem(y + ky, NY), body)

    loop(NY, scatter_x)
    mean = mean_v[...]
    c_v[...] = dot(mean, mean, ((0,), (0,)), lax.Precision.HIGHEST)

    def scatter_y(i):
        ky = far_first(i, NY)

        def body(start, size):
            part = span(start, size)
            value = qp_v[whole(x, start, size), :]
            for kx in range(NX - 1):
                wait(rx_rx.at[kx, part], rx_r.at[kx, ky])
                value = value + rx_rx[kx, part, :]
            ry_v[part, :] = value

            @pl.when(ky > 0)
            def _():
                dst = ry_rx.at[ky - 1, pl.ds(0, size)]
                send(ry_v.at[part], dst, ry_s, ry_r.at[ky - 1], along_y(i)[1])

        for_piece(lax.rem(y + ky, NY), body)

    steps = rank // 8

    def stage(i):
        first = jnp.where(i == 0, 0, FIRST + i - 1)
        last = jnp.where(i == NY, steps, FIRST + i)
        c_v[...] = lax.fori_loop(first, last, panel, c_v[...])

        @pl.when(i < NY)
        def _():
            scatter_y(i)

    loop(NY + 1, stage)
    inverse = inverse_factor(c_v[...])

    def to_x(ref):
        loop(NX - 1, lambda j: send(ref, ref, gx_s, gx_r, along_x(j)[2]))

    def gather_own(start, size):
        def add(i, value):
            wait(ry_rx.at[i, pl.ds(0, size)], ry_r.at[i])
            return value + ry_rx[i, :size]

        total = lax.fori_loop(0, NY - 1, add, ry_v[span(start, size), :])
        right_v[whole(x, start, size), :] = times_transposed(total, inverse) / replicas
        out = right_v.at[whole(x, start, size)]
        to_x(out)
        loop(NY - 1, lambda i: send(out, out, gy_s, gy_r.at[along_y(i)[0] - 1], along_y(i)[1]))

    for_piece(y, gather_own)
    p_hat_out[...] = times_transposed(mean_v[...], inverse)
    sent = qp_v.at[pl.ds(0, (NX - 1) * cols)]
    wait(sent, rx_s)

    def pass_on(i):
        ky = far_first(NY - 2 - i, NY)

        def body(start, size):
            got = right_v.at[whole(x, start, size)]
            wait(got, gy_r.at[ky - 1])
            to_x(got)

        for_piece(lax.rem(y + NY - ky, NY), body)

    loop(NY - 1, pass_on)

    def sent_along_y(start, size):
        wait(ry_v.at[pl.ds(0, cols - size)], ry_s)
        wait(qp_v.at[pl.ds(0, (NY - 1) * size)], gy_s)

    for_piece(y, sent_along_y)
    wait(sent, gx_r)
    wait(sent, gx_s)
    right_out[...] = right_v[...]


def finish(
    m_v, q_v, p_hat_v, approx_hbm, q_hbm, error_hbm,
    p3_v, approx_v, error_v, q_sem, sems,
):
    _, rows, width = m_v.shape
    q_copy = pltpu.make_async_copy(q_v, q_hbm, q_sem)
    q_copy.start()
    high, low = halves(p_hat_v[...])
    p3_v[...] = jnp.concatenate([high, low, high], axis=1)

    def stores(i, columns):
        return [
            pltpu.make_async_copy(src.at[:, columns], dst.at[:, columns], sems.at[k, i])
            for k, (src, dst) in enumerate(((approx_v, approx_hbm), (error_v, error_hbm)))
        ]

    def tile(i, columns):
        high, low = halves(q_v[columns, :])
        full = dot(p3_v[...], jnp.concatenate([high, high, low], axis=1), ((1,), (1,)))
        approx_v[:, columns] = full.astype(BF16)
        error_v[:, columns] = (m_v[0, :, columns].astype(F32) + m_v[1, :, columns].astype(F32) - full).astype(BF16)
        for copy in stores(i, columns):
            copy.start()

    tiles = width // WIDE
    rest = pl.ds(tiles * WIDE, width - tiles * WIDE)
    tile(tiles, rest)
    loop(tiles, lambda i: tile(i, span(i * WIDE, WIDE, 128)))
    loop(tiles, lambda i: [copy.wait() for copy in stores(i, span(i * WIDE, WIDE, 128))])
    for copy in stores(tiles, rest):
        copy.wait()
    q_copy.wait()


def local(grads, errors, q_start):
    grads, errors = grads[0], errors[0]
    rows, width = grads.shape
    rank = q_start.shape[1]
    chunk = rows // (NX * NC)
    cols = width // NX
    nxc = NX * NC - 1
    anywhere = pl.BlockSpec(memory_space=pl.ANY)
    vmem = pl.BlockSpec(memory_space=pltpu.VMEM)
    dma = pltpu.SemaphoreType.DMA
    merged, right, p_hat = pl.pallas_call(
        exchange,
        out_shape=(
            pltpu.VMEM((2, rows, width), BF16),
            pltpu.VMEM((width, rank), F32),
            pltpu.VMEM((rows, rank), F32),
        ),
        in_specs=[anywhere] * 3,
        out_specs=(vmem,) * 3,
        scratch_shapes=[
            pltpu.VMEM((width, rank), F32),
            pltpu.VMEM((2, width, rows), BF16),
            pltpu.VMEM((rows, rank), F32),
            pltpu.VMEM((nxc, chunk, rank), F32),
            pltpu.VMEM((NY, SPLIT, rank), F32),
            pltpu.VMEM((NZ, chunk - SPLIT, rank), F32),
            pltpu.VMEM((NZ, SPLIT, rank), F32),
            pltpu.VMEM((NY, chunk - SPLIT, rank), F32),
            pltpu.VMEM((rows, rank), F32),
            pltpu.VMEM((rows, 2 * rank), BF16),
            pltpu.VMEM((width, rank), F32),
            pltpu.VMEM((NX - 1, cols, rank), F32),
            pltpu.VMEM((cols, rank), F32),
            pltpu.VMEM((NY - 1, LONG, rank), F32),
            pltpu.VMEM((width, rank), F32),
            pltpu.VMEM((rank, rank), F32),
            dma, dma((2, rows // BLOCK)),
            dma, dma((nxc,)),
            dma, dma, dma, dma, dma, dma, dma, dma,
            dma, dma,
            dma, dma((NX - 1, NY)),
            dma, dma((NY - 1,)),
            dma, dma((NY - 1,)),
            dma, dma,
        ],
        compiler_params=pltpu.CompilerParams(collective_id=0, has_side_effects=True, vmem_limit_bytes=LIMIT),
        name="exchange",
    )(grads, errors, q_start)

    approx, q_next, error_next = pl.pallas_call(
        finish,
        out_shape=(
            jax.ShapeDtypeStruct((rows, width), BF16),
            jax.ShapeDtypeStruct((width, rank), F32),
            jax.ShapeDtypeStruct((rows, width), BF16),
        ),
        in_specs=[vmem] * 3,
        out_specs=(anywhere,) * 3,
        scratch_shapes=[
            pltpu.VMEM((rows, 3 * rank), BF16),
            pltpu.VMEM((rows, width), BF16),
            pltpu.VMEM((rows, width), BF16),
            dma,
            dma((2, width // WIDE + 1)),
        ],
        compiler_params=pltpu.CompilerParams(vmem_limit_bytes=LIMIT - 2**20),
        name="finish",
    )(merged, right, p_hat)
    return approx, q_next, error_next[None]


def solution(mesh):
    return jax.shard_map(
        local,
        mesh=mesh,
        in_specs=(P("dp", None, "mp"), P("dp", None, "mp"), P("mp", None)),
        out_specs=(P(None, "mp"), P("mp", None), P("dp", None, "mp")),
        check_vma=False,
    )
```
